512 devices in a mesh: dom: 512 (over z, y, x, core).
Axes of the slice: x: 4, y: 8, z: 8, core: 2. Of those that a mesh axis runs over, the one named last changes fastest.
Arguments:
- node_feats: bfloat16 [524288, 256], P('dom'), may hold values from -6 to 6
- send_index: int32 [512, 4, 128], P('dom'), may hold values from 0 to 1023, as said below
- send_count: int32 [512, 4], P('dom'), may hold values from 1 to 128
- tile_cols: int32 [4096, 8], P('dom'), may hold values from 0 to 11, as said below
- tile_vals: bfloat16 [4096, 8, 128, 128], P('dom'), may hold values from -0.1875 to 0.1875
- w_self: bfloat16 [256, 256], replicated, may hold values from -0.375 to 0.375
- w_neigh: bfloat16 [256, 256], replicated, may hold values from -0.375 to 0.375
- grad_out: bfloat16 [524288, 256], P('dom'), may hold values from -6 to 6
Outputs:
- node_out: bfloat16 [524288, 256], P('dom')
- grad_nodes: bfloat16 [524288, 256], P('dom')
- grad_w_self: float32 [256, 256], replicated
- grad_w_neigh: float32 [256, 256], replicated
The draws below stay inside these ranges and needn't reach their ends.
Inputs may be any that keep to these rules, and one draw needn't show every extreme that they name: `send_index`: the 128 entries of one list name distinct local rows. `tile_cols`: the first entry of each block row is that block row's own index within its partition.
All inputs are finite; a program needn't handle non-finite values.
Results may differ from the reference program's by a relative error of at most 0.0061.
Values may be sent and summed in bfloat16 or wider, within the bound.
No kernel may reach another device: no remote copies, remote signals or barrier semaphores. Data moves between devices by JAX's collectives and lax.ppermute only.
A program may use at most 64 MiB of HBM per device.

```python
import jax
import jax.numpy as jnp
from jax import lax

F = 256
H = 256
TILE = 128
TPB = 8
CAP = 128
ROWS_DEV = 1024
BLOCK_ROWS = 8
EXT_BLOCKS = 12
NODES = 524288
N_DOM = 512


def draw_send_index(key, part):
    key = jax.random.fold_in(key, 11)
    subkeys = jax.random.split(key, N_DOM * 4)
    chosen = jax.vmap(lambda subkey: jax.random.permutation(subkey, ROWS_DEV)[:CAP])(subkeys)
    return chosen.reshape(N_DOM, 4, CAP).astype(jnp.int32)


def draw_send_count(key, part):
    key = jax.random.fold_in(key, 12)
    first_key, second_key = jax.random.split(key)
    counts = jax.random.randint(first_key, (N_DOM * 4,), 1, CAP + 1)
    fullest = jax.random.randint(second_key, (), 0, N_DOM * 4)
    counts = jnp.where(jnp.arange(N_DOM * 4) == fullest, CAP, counts)
    return counts.reshape(N_DOM, 4).astype(jnp.int32)


def draw_tile_cols(key, part):
    key = jax.random.fold_in(key, 13)
    total_blocks = N_DOM * BLOCK_ROWS
    picks = jax.random.randint(key, (total_blocks, TPB), 0, EXT_BLOCKS)
    own_block = jnp.arange(total_blocks, dtype=jnp.int32) % BLOCK_ROWS
    return picks.at[:, 0].set(own_block).astype(jnp.int32)


def steps_of(stream_key, extent, cuts, low, largest):
    level = 1.0
    for dim, parts in cuts:
        draws = jax.random.uniform(jax.random.fold_in(jax.random.fold_in(stream_key, 6), dim), (parts,), jnp.float32, low / len(cuts), largest / len(cuts))
        level = level * jnp.repeat(jnp.exp(draws), extent[dim] // parts).reshape((-1,) + (1,) * (len(extent) - 1 - dim))
    return level


def scatter_about(own_key, extent, scale, limit, cuts=(), kind=jnp.bfloat16):
    gain = steps_of(own_key, extent, cuts, -0.22, 0.18) if cuts else 1.0
    array = jax.random.normal(own_key, extent, jnp.float32) * scale * gain
    return jnp.minimum(jnp.maximum(array, -limit), limit).astype(kind)


def setup_inputs(seed: int = 0) -> dict:
    arg_keys = jax.random.split(jax.random.key(seed), 9)
    return {
        "node_feats": scatter_about(arg_keys[0], (NODES, F), 1.0, 6.0, ((0, 512),)),
        "send_index": draw_send_index(jax.random.fold_in(arg_keys[8], 71), 0),
        "send_count": draw_send_count(jax.random.fold_in(arg_keys[8], 71), 0),
        "tile_cols": draw_tile_cols(jax.random.fold_in(arg_keys[8], 71), 0),
        "tile_vals": scatter_about(arg_keys[4], (NODES // TILE, TPB, TILE, TILE), (TILE * TPB) ** -0.5, 0.1875, ((0, 512),)),
        "w_self": scatter_about(arg_keys[5], (F, H), F ** -0.5, 0.375),
        "w_neigh": scatter_about(arg_keys[6], (F, H), F ** -0.5, 0.375),
        "grad_out": scatter_about(arg_keys[7], (NODES, H), 1.0, 6.0, ((0, 512),)),
    }


OFFSETS = (1, -1, 2, -2)


def silu_slope(preact):
    sigmoid_v = jax.nn.sigmoid(preact)
    return sigmoid_v * (1.0 + preact * (1.0 - sigmoid_v))


def partition_step(items, w_self, w_neigh):
    own_rows, arrived, cols_local, vals_local, grad_local = items
    extended = jnp.concatenate([own_rows, arrived.reshape(4 * CAP, F)], axis=0)
    picked = extended.reshape(EXT_BLOCKS, TILE, F)[cols_local]
    aggregate = jnp.einsum("rtij,rtjf->rif", vals_local.astype(jnp.float32), picked.astype(jnp.float32),
                           precision=lax.Precision.HIGHEST).reshape(ROWS_DEV, F).astype(jnp.bfloat16)
    preact = jnp.dot(own_rows, w_self, preferred_element_type=jnp.float32) + jnp.dot(aggregate, w_neigh, preferred_element_type=jnp.float32)
    node_out = jax.nn.silu(preact).astype(jnp.bfloat16)
    grad_pre = (grad_local.astype(jnp.float32) * silu_slope(preact)).astype(jnp.bfloat16)
    part_self = jnp.dot(own_rows.T, grad_pre, preferred_element_type=jnp.float32)
    part_neigh = jnp.dot(aggregate.T, grad_pre, preferred_element_type=jnp.float32)
    grad_agg = jnp.dot(grad_pre, w_neigh.T, preferred_element_type=jnp.float32).astype(jnp.bfloat16)
    grad_self = jnp.dot(grad_pre, w_self.T, preferred_element_type=jnp.float32)
    contrib = jnp.einsum("rtij,rif->rtjf", vals_local.astype(jnp.float32),
                         grad_agg.reshape(BLOCK_ROWS, TILE, F).astype(jnp.float32), precision=lax.Precision.HIGHEST)
    grad_ext = jax.ops.segment_sum(contrib.reshape(BLOCK_ROWS * TPB, TILE, F), cols_local.reshape(-1),
                                   num_segments=EXT_BLOCKS).reshape(ROWS_DEV + 4 * CAP, F)
    own_grad = grad_self + grad_ext[:ROWS_DEV]
    grad_back = grad_ext[ROWS_DEV:].reshape(4, CAP, F).astype(jnp.bfloat16)
    return node_out, own_grad, part_self, part_neigh, grad_back


def reference(node_feats, send_index, send_count, tile_cols, tile_vals, w_self, w_neigh, grad_out):
    feat_local = node_feats.reshape(N_DOM, ROWS_DEV, F)
    slot_ids = jnp.arange(CAP, dtype=jnp.int32)
    live = slot_ids[None, None, :] < send_count[:, :, None]
    chosen = jax.vmap(lambda block, index: block[index])(feat_local, send_index)
    payload = jnp.where(live[..., None], chosen, jnp.zeros((), jnp.bfloat16))
    position = jnp.arange(N_DOM, dtype=jnp.int32)
    received = []
    for slot_num in range(4):
        source = position - OFFSETS[slot_num]
        valid = (source >= 0) & (source < N_DOM)
        taken = payload[jnp.clip(source, 0, N_DOM - 1), slot_num]
        received.append(jnp.where(valid[:, None, None], taken, jnp.zeros((), jnp.bfloat16)))
    arrived = jnp.stack(received, axis=1)
    items = (feat_local, arrived, tile_cols.reshape(N_DOM, BLOCK_ROWS, TPB),
             tile_vals.reshape(N_DOM, BLOCK_ROWS, TPB, TILE, TILE), grad_out.reshape(N_DOM, ROWS_DEV, H))
    node_out, own_grad, part_self, part_neigh, grad_back = lax.map(lambda its: partition_step(its, w_self, w_neigh), items)
    scale = float(NODES) ** -0.5
    grad_w_self = jnp.sum(part_self, axis=0) * scale
    grad_w_neigh = jnp.sum(part_neigh, axis=0) * scale
    for slot_num in range(4):
        target = position + OFFSETS[slot_num]
        valid = (target >= 0) & (target < N_DOM)
        coming = grad_back[jnp.clip(target, 0, N_DOM - 1), slot_num].astype(jnp.float32)
        coming = jnp.where(valid[:, None, None] & live[:, slot_num, :, None], coming, 0.0)
        own_grad = jax.vmap(lambda total, index, values: total.at[index].add(values))(own_grad, send_index[:, slot_num], coming)
    grad_nodes = own_grad.reshape(NODES, F).astype(jnp.bfloat16)
    return node_out.reshape(NODES, H), grad_nodes, grad_w_self, grad_w_neigh
```

```python
import jax
import jax.numpy as jnp
from jax import lax
from jax.sharding import Mesh, PartitionSpec as P

OFFSETS = (1, -1, 2, -2)
DOM = ("z", "y", "x", "core")
ROW = ("x", "core")


def exchange(value, axes):
    return lax.all_to_all(value, axes, 0, 0, tiled=False)


def total_over_dom(part):
    rows, cols = part.shape
    row_n, y_n, z_n = lax.axis_size(ROW), lax.axis_size("y"), lax.axis_size("z")
    share = exchange(part.astype(jnp.bfloat16).reshape(row_n, rows // row_n, cols), ROW)
    share = share.astype(jnp.float32).sum(0).astype(jnp.bfloat16)
    share = exchange(jnp.broadcast_to(share, (y_n,) + share.shape), "y")
    share = share.astype(jnp.float32).sum(0)
    share = exchange(jnp.broadcast_to(share, (z_n,) + share.shape), "z").sum(0)
    return share


def gather_row(share):
    row_n = lax.axis_size(ROW)
    share = share.astype(jnp.bfloat16)
    whole = exchange(jnp.broadcast_to(share, (row_n,) + share.shape), ROW)
    return whole.reshape(row_n * share.shape[0], share.shape[1]).astype(jnp.float32)


def shifted(value, axis, steps):
    count = lax.axis_size(axis)
    first, last = (max(0, -steps), min(count, count - steps))
    return lax.ppermute(value, axis, [(source, source + steps) for source in range(first, last)])


def silu_slope(preact):
    sigmoid_v = jax.nn.sigmoid(preact)
    return sigmoid_v * (1.0 + preact * (1.0 - sigmoid_v))


def shards(node_feats, send_index, send_count, tile_cols, tile_vals, w_self, w_neigh, grad_out):
    row_count, feat_width = node_feats.shape
    tile_size = tile_vals.shape[2]
    block_rows, row_tiles = tile_cols.shape
    capacity = send_index.shape[2]
    slot_ids = jnp.arange(capacity, dtype=jnp.int32)
    live = [(slot_ids < send_count[0, slot_num])[:, None] for slot_num in range(4)]
    payload = [
        jnp.where(live[slot_num], node_feats[send_index[0, slot_num]], jnp.zeros((), jnp.bfloat16))
        for slot_num in range(4)
    ]
    arrived = [shifted(payload[slot_num], DOM, OFFSETS[slot_num]) for slot_num in range(4)]
    extended = jnp.concatenate([node_feats] + arrived, axis=0)
    ext_count = extended.shape[0] // tile_size
    picked = extended.reshape(ext_count, tile_size, feat_width)[tile_cols]
    aggregate = jnp.einsum("rtij,rtjf->rif", tile_vals, picked, preferred_element_type=jnp.float32)
    aggregate = aggregate.reshape(row_count, feat_width).astype(jnp.bfloat16)
    preact = jnp.dot(node_feats, w_self, preferred_element_type=jnp.float32) + jnp.dot(
        aggregate, w_neigh, preferred_element_type=jnp.float32
    )
    node_out = jax.nn.silu(preact).astype(jnp.bfloat16)
    grad_pre = (grad_out.astype(jnp.float32) * silu_slope(preact)).astype(jnp.bfloat16)
    part_self = jnp.einsum("nf,nh->fh", node_feats, grad_pre, preferred_element_type=jnp.float32)
    part_neigh = jnp.einsum("nf,nh->fh", aggregate, grad_pre, preferred_element_type=jnp.float32)
    scale = float(row_count * lax.axis_size(DOM)) ** (-0.5)
    summed = gather_row(total_over_dom(jnp.concatenate([part_self, part_neigh])) * scale)
    grad_agg = jnp.einsum(
        "nh,fh->nf", grad_pre, w_neigh, preferred_element_type=jnp.float32
    ).astype(jnp.bfloat16)
    grad_self = jnp.einsum("nh,fh->nf", grad_pre, w_self, preferred_element_type=jnp.float32)
    contrib = jnp.einsum(
        "rtij,rif->rtjf",
        tile_vals,
        grad_agg.reshape(block_rows, tile_size, feat_width),
        preferred_element_type=jnp.float32,
    )
    grad_ext = (
        jnp.zeros((ext_count, tile_size, feat_width), jnp.float32)
        .at[tile_cols.reshape(-1)]
        .add(contrib.reshape(block_rows * row_tiles, tile_size, feat_width))
    )
    grad_ext = grad_ext.reshape(ext_count * tile_size, feat_width)
    regions = [
        grad_ext[row_count + slot_num * capacity : row_count + (slot_num + 1) * capacity].astype(
            jnp.bfloat16
        )
        for slot_num in range(4)
    ]
    returned = [shifted(regions[slot_num], DOM, -OFFSETS[slot_num]) for slot_num in range(4)]
    total = grad_self + grad_ext[:row_count]
    for slot_num in range(4):
        incoming = jnp.where(live[slot_num], returned[slot_num].astype(jnp.float32), 0.0)
        total = total.at[send_index[0, slot_num]].add(incoming)
    grad_nodes = total.astype(jnp.bfloat16)
    return (node_out, grad_nodes, summed[:feat_width], summed[feat_width:])


def solution(mesh):
    grid = Mesh(mesh.devices.reshape(4, 8, 8, 2), DOM)
    placed = (
        P(DOM, None),
        P(DOM, None, None),
        P(DOM, None),
        P(DOM, None),
        P(DOM, None, None, None),
        P(),
        P(),
        P(DOM, None),
    )
    return jax.shard_map(
        shards,
        mesh=grid,
        in_specs=placed,
        out_specs=(P(DOM, None), P(DOM, None), P(), P()),
        check_vma=False,
    )
```

```python
import jax
import jax.numpy as jnp
from jax import lax
from jax.experimental import pallas as pl
from jax.experimental.pallas import tpu as pltpu
from jax.sharding import Mesh, PartitionSpec as P

OFFSETS = (1, -1, 2, -2)
DOM = ("z", "y", "x", "core")
ROW = ("x", "core")
TILE = 128
VMEM_BYTES = 40 * 1024 * 1024


def product(left, right, left_dim=1, right_dim=0):
    return lax.dot_general(
        left, right, (((left_dim,), (right_dim,)), ((), ())), preferred_element_type=jnp.float32
    )


def ahead(value):
    return lax.optimization_barrier(value)


def exchange(value, axes):
    return lax.all_to_all(value, axes, 0, 0, tiled=False)


def shifted(value, steps):
    count = lax.axis_size(DOM)
    first, last = (max(0, -steps), min(count, count - steps))
    return lax.ppermute(value, DOM, [(source, source + steps) for source in range(first, last)])


def listed_rows(index_ref, count_ref, slot):
    indices = index_ref[0, slot : slot + 1, :]
    lane = lax.broadcasted_iota(jnp.int32, indices.shape, 1)
    return jnp.where(lane < count_ref[0, slot], indices, -1)


def payload_kernel(index_ref, count_ref, feats_ref, *out_refs):
    rows = feats_ref.shape[0]
    for slot in range(4):
        indices = listed_rows(index_ref, count_ref, slot)
        column = jnp.transpose(jnp.broadcast_to(indices, (TILE, TILE)))
        place = lax.broadcasted_iota(jnp.int32, (TILE, TILE), 1)
        chosen = jnp.concatenate(
            [(column == place + block * TILE).astype(jnp.bfloat16) for block in range(rows // TILE)], axis=1
        )
        out_refs[slot][...] = product(chosen, feats_ref[...]).astype(jnp.bfloat16)


def payloads(send_index, send_count, node_feats):
    shape = jax.ShapeDtypeStruct((TILE, node_feats.shape[1]), jnp.bfloat16)
    vmem = pl.BlockSpec(memory_space=pltpu.VMEM)
    return pl.pallas_call(
        payload_kernel,
        out_shape=[shape] * 4,
        in_specs=[vmem, pl.BlockSpec(memory_space=pltpu.SMEM), vmem],
        out_specs=[vmem] * 4,
        compiler_params=pltpu.CompilerParams(vmem_limit_bytes=VMEM_BYTES),
        cost_estimate=pl.CostEstimate(flops=2 * 512 * 1024 * 256, bytes_accessed=1 << 20, transcendentals=0),
        name="payload",
    )(send_index, send_count, node_feats)


def layer_kernel(
    cols_ref, feats_hbm, got0, got1, got2, got3, vals_hbm, w_self_ref, w_neigh_ref, grad_out_ref,
    node_out_ref, own_grad_ref, parts_ref, back0, back1, back2, back3,
    ext, vals, agg, grad_pre, grad_ext, ext_sem, vals_sem,
):
    blocks, tiles = cols_ref.shape
    rows = feats_hbm.shape[0]
    copies = [pltpu.make_async_copy(feats_hbm, ext.at[0:rows], ext_sem.at[0])]
    for slot, got in enumerate((got0, got1, got2, got3)):
        low = rows + slot * TILE
        copies.append(pltpu.make_async_copy(got, ext.at[low : low + TILE], ext_sem.at[slot + 1]))
    val_copies = [pltpu.make_async_copy(vals_hbm.at[r], vals.at[r], vals_sem.at[r]) for r in range(blocks)]
    for copy in copies:
        copy.start()
    for copy in val_copies:
        copy.start()
    grad_ext[...] = jnp.zeros_like(grad_ext)
    for copy in copies:
        copy.wait()

    def block_at(r, t):
        return pl.ds(pl.multiple_of(cols_ref[r, t] * TILE, TILE), TILE)

    for r in range(blocks):
        span = pl.ds(r * TILE, TILE)
        val_copies[r].wait()
        tile_row = jnp.concatenate([vals[r, t] for t in range(tiles)], axis=1)
        picked = jnp.concatenate([ext[block_at(r, t), :] for t in range(tiles)], axis=0)
        aggregate = product(tile_row, picked).astype(jnp.bfloat16)
        agg[span, :] = aggregate
        preact = product(ext[span, :], w_self_ref[...]) + product(aggregate, w_neigh_ref[...])
        sigma = 1.0 / (1.0 + jnp.exp(-preact))
        node_out_ref[span, :] = (preact * sigma).astype(jnp.bfloat16)
        slope = sigma * (1.0 + preact * (1.0 - sigma))
        grad = (grad_out_ref[span, :].astype(jnp.float32) * slope).astype(jnp.bfloat16)
        grad_pre[span, :] = grad
        own_grad_ref[span, :] = product(grad, w_self_ref[...], 1, 1)
        grad_agg = product(grad, w_neigh_ref[...], 1, 1).astype(jnp.bfloat16)
        contrib = product(tile_row, grad_agg, 0, 0)
        for t in range(tiles):
            grad_ext[block_at(r, t), :] += contrib[t * TILE : (t + 1) * TILE, :]
    width = parts_ref.shape[0] // 2
    parts_ref[0:width, :] = product(ext[0:rows, :], grad_pre[...], 0, 0).astype(jnp.bfloat16)
    parts_ref[width:, :] = product(agg[...], grad_pre[...], 0, 0).astype(jnp.bfloat16)
    own_grad_ref[...] += grad_ext[0:rows, :]
    for slot, back in enumerate((back0, back1, back2, back3)):
        low = rows + slot * TILE
        back[...] = grad_ext[low : low + TILE, :].astype(jnp.bfloat16)


def layer(tile_cols, node_feats, arrived, tile_vals, w_self, w_neigh, grad_out):
    rows, width = node_feats.shape
    ext_rows = rows + 4 * TILE
    vmem, hbm = pl.BlockSpec(memory_space=pltpu.VMEM), pl.BlockSpec(memory_space=pl.ANY)
    out_shape = [
        jax.ShapeDtypeStruct((rows, width), jnp.bfloat16),
        jax.ShapeDtypeStruct((rows, width), jnp.float32),
        jax.ShapeDtypeStruct((2 * width, width), jnp.bfloat16),
    ] + [jax.ShapeDtypeStruct((TILE, width), jnp.bfloat16)] * 4
    return pl.pallas_call(
        layer_kernel,
        out_shape=out_shape,
        in_specs=[pl.BlockSpec(memory_space=pltpu.SMEM)] + [hbm] * 6 + [vmem] * 3,
        out_specs=[vmem] * 7,
        scratch_shapes=[
            pltpu.VMEM((ext_rows, width), jnp.bfloat16),
            pltpu.VMEM(tile_vals.shape, jnp.bfloat16),
            pltpu.VMEM((rows, width), jnp.bfloat16),
            pltpu.VMEM((rows, width), jnp.bfloat16),
            pltpu.VMEM((ext_rows, width), jnp.float32),
            pltpu.SemaphoreType.DMA((5,)),
            pltpu.SemaphoreType.DMA((tile_cols.shape[0],)),
        ],
        compiler_params=pltpu.CompilerParams(vmem_limit_bytes=VMEM_BYTES),
        cost_estimate=pl.CostEstimate(flops=2 << 30, bytes_accessed=6 << 20, transcendentals=1 << 18),
        name="layer",
    )(tile_cols, node_feats, *arrived, tile_vals, w_self, w_neigh, grad_out)


def collect_kernel(index_ref, count_ref, own_ref, back0, back1, back2, back3, out_ref):
    rows = own_ref.shape[0]
    returned = jnp.concatenate([back0[...], back1[...], back2[...], back3[...]], axis=0)
    listed = [
        jnp.broadcast_to(listed_rows(index_ref, count_ref, slot), (TILE, TILE)) for slot in range(4)
    ]
    for block in range(rows // TILE):
        span = pl.ds(block * TILE, TILE)
        place = lax.broadcasted_iota(jnp.int32, (TILE, TILE), 0) + block * TILE
        chosen = jnp.concatenate([(row == place).astype(jnp.bfloat16) for row in listed], axis=1)
        out_ref[span, :] = (own_ref[span, :] + product(chosen, returned)).astype(jnp.bfloat16)


def collect(send_index, send_count, own_grad, returned):
    vmem = pl.BlockSpec(memory_space=pltpu.VMEM)
    return pl.pallas_call(
        collect_kernel,
        out_shape=jax.ShapeDtypeStruct(own_grad.shape, jnp.bfloat16),
        in_specs=[vmem, pl.BlockSpec(memory_space=pltpu.SMEM)] + [vmem] * 5,
        out_specs=vmem,
        compiler_params=pltpu.CompilerParams(vmem_limit_bytes=VMEM_BYTES),
        cost_estimate=pl.CostEstimate(flops=2 * 512 * 1024 * 256, bytes_accessed=2 << 20, transcendentals=0),
        name="collect",
    )(send_index, send_count, own_grad, *returned)


def copies_for(share, axes):
    return jnp.broadcast_to(share, (lax.axis_size(axes),) + share.shape)


def shards(node_feats, send_index, send_count, tile_cols, tile_vals, w_self, w_neigh, grad_out):
    rows, width = node_feats.shape
    payload = payloads(send_index, send_count, node_feats)
    arrived = [shifted(payload[slot], OFFSETS[slot]) for slot in range(4)]
    node_out, own_grad, parts, *back = layer(
        tile_cols, node_feats, arrived, tile_vals, w_self, w_neigh, grad_out
    )
    returned = [shifted(back[slot], -OFFSETS[slot]) for slot in range(4)]
    row_n = lax.axis_size(ROW)
    share = exchange(parts.reshape(row_n, 2 * width // row_n, width), ROW)
    share = share.astype(jnp.float32).sum(0).astype(jnp.bfloat16)
    share = exchange(copies_for(share, "y"), "y").astype(jnp.float32).sum(0)
    share = exchange(copies_for(share, "z"), "z").sum(0)
    share = (share * float(rows * lax.axis_size(DOM)) ** (-0.5)).astype(jnp.bfloat16)
    share, *returned = ahead((share, *returned))
    whole = exchange(copies_for(share, ROW), ROW).reshape(2 * width, width)
    grad_nodes = collect(send_index, send_count, own_grad, returned)
    return (
        node_out,
        grad_nodes,
        whole[:width].astype(jnp.float32),
        whole[width:].astype(jnp.float32),
    )


def solution(mesh):
    grid = Mesh(mesh.devices.reshape(4, 8, 8, 2), DOM)
    placed = (
        P(DOM, None),
        P(DOM, None, None),
        P(DOM, None),
        P(DOM, None),
        P(DOM, None, None, None),
        P(),
        P(),
        P(DOM, None),
    )
    return jax.shard_map(
        shards,
        mesh=grid,
        in_specs=placed,
        out_specs=(P(DOM, None), P(DOM, None), P(), P()),
        check_vma=False,
    )
```

```python
import functools

import jax
import jax.numpy as jnp
from jax import lax
from jax.experimental import pallas as pl
from jax.experimental.pallas import tpu as pltpu
from jax.sharding import Mesh, PartitionSpec as P

DOM = ("z", "y", "x", "core")
ROW = ("x", "core")
TILE = 128
PARAMS = pltpu.CompilerParams(vmem_limit_bytes=60 * 1024 * 1024)
VMEM = pl.BlockSpec(memory_space=pltpu.VMEM)
HBM = pl.BlockSpec(memory_space=pltpu.HBM)
ANY = pl.BlockSpec(memory_space=pl.ANY)


def product(left, right, left_dim=1, right_dim=0):
    return lax.dot_general(
        left, right, (((left_dim,), (right_dim,)), ((), ())), preferred_element_type=jnp.float32
    )


def exchange(value, axes):
    return lax.all_to_all(value, axes, 0, 0, tiled=False)


def copies_for(share, axes):
    return jnp.broadcast_to(share, (lax.axis_size(axes),) + share.shape)


def swapped(value):
    return lax.ppermute(value, "core", [(0, 1), (1, 0)])


def shifted(value, steps):
    count = lax.axis_size(DOM)
    first, last = (max(0, -steps), min(count, count - steps))
    return lax.ppermute(value, DOM, [(source, source + steps) for source in range(first, last)])


def started(*pairs):
    copies = [pltpu.make_async_copy(*pair) for pair in pairs]
    for copy in copies:
        copy.start()
    return copies


def listed_rows(index_ref, count_ref, slot):
    indices = index_ref[0, slot : slot + 1, :]
    lane = lax.broadcasted_iota(jnp.int32, indices.shape, 1)
    return jnp.where(lane < count_ref[0, slot], indices, -1)


def payload_kernel(index_hbm, count_hbm, feats_hbm, swap_ref, up_ref, down_ref, index, count, feats, sems):
    rows = feats.shape[0]
    index_copy, count_copy, feats_copy = started(
        (index_hbm, index, sems.at[0]), (count_hbm, count, sems.at[1]), (feats_hbm, feats, sems.at[2])
    )
    index_copy.wait()
    count_copy.wait()
    place = lax.broadcasted_iota(jnp.int32, (TILE, TILE), 1)
    chosen = []
    for slot in range(4):
        column = jnp.transpose(jnp.broadcast_to(listed_rows(index, count, slot), (TILE, TILE)))
        chosen.append(
            jnp.concatenate(
                [(column == place + block * TILE).astype(jnp.bfloat16) for block in range(rows // TILE)], axis=1
            )
        )
    feats_copy.wait()
    picked = product(jnp.concatenate(chosen, axis=0), feats[...]).astype(jnp.bfloat16)
    swap_ref[...] = picked[0 : 2 * TILE]
    up_ref[...] = picked[2 * TILE : 3 * TILE]
    down_ref[...] = picked[3 * TILE :]


def payloads(send_index, send_count, node_feats):
    width = node_feats.shape[1]
    return pl.pallas_call(
        payload_kernel,
        out_shape=[jax.ShapeDtypeStruct((size, width), jnp.bfloat16) for size in (2 * TILE, TILE, TILE)],
        in_specs=[HBM] * 3,
        out_specs=[VMEM] * 3,
        scratch_shapes=[
            pltpu.VMEM(send_index.shape, jnp.int32),
            pltpu.SMEM(send_count.shape, jnp.int32),
            pltpu.VMEM(node_feats.shape, jnp.bfloat16),
            pltpu.SemaphoreType.DMA((3,)),
        ],
        compiler_params=PARAMS,
        cost_estimate=pl.CostEstimate(flops=2 * 512 * 1024 * 256, bytes_accessed=1 << 20, transcendentals=0),
        name="payload",
    )(send_index, send_count, node_feats)


def join_kernel(for_up, up_ref, down_ref, swap_ref, first_ref, second_ref):
    first_ref[0:TILE, :] = up_ref[...]
    first_ref[TILE:, :] = swap_ref[for_up * TILE : (for_up + 1) * TILE, :]
    second_ref[0:TILE, :] = down_ref[...]
    second_ref[TILE:, :] = swap_ref[(1 - for_up) * TILE : (2 - for_up) * TILE, :]


def joined(up, down, swap, for_up):
    return pl.pallas_call(
        functools.partial(join_kernel, for_up),
        out_shape=[jax.ShapeDtypeStruct((2 * TILE, up.shape[1]), up.dtype)] * 2,
        in_specs=[VMEM] * 3,
        out_specs=[VMEM] * 2,
        compiler_params=pltpu.CompilerParams(vmem_limit_bytes=4 * 1024 * 1024),
        name="join",
    )(up, down, swap)


def forward_kernel(
    cols_hbm, feats_hbm, swap_hbm, up_hbm, down_hbm, vals_hbm, w_self_hbm, w_neigh_hbm, grad_out_hbm,
    node_out_hbm, grad_pre, parts_ref,
    cols, ext, vals, agg, w_self, w_neigh, grad_out, node_out, sems, vals_sem,
):
    blocks, tiles = cols.shape
    rows, width = grad_out.shape
    val_copies = started(*[(vals_hbm.at[r], vals.at[r], vals_sem.at[r]) for r in range(blocks)])
    slots = [ext.at[rows + slot * TILE : rows + (slot + 1) * TILE] for slot in range(4)]
    head, tail = pl.ds(0, TILE), pl.ds(TILE, TILE)
    first = started(
        (cols_hbm, cols, sems.at[0]),
        (feats_hbm, ext.at[0:rows], sems.at[1]),
        (up_hbm.at[head], slots[2], sems.at[4]),
        (down_hbm.at[head], slots[3], sems.at[5]),
    )
    later = started(
        (w_self_hbm, w_self, sems.at[6]), (w_neigh_hbm, w_neigh, sems.at[7]), (grad_out_hbm, grad_out, sems.at[8])
    )
    core = lax.axis_index("core")

    @pl.when(core == 0)
    def _():
        started((up_hbm.at[tail], slots[0], sems.at[2]), (swap_hbm.at[tail], slots[1], sems.at[3]))

    @pl.when(core != 0)
    def _():
        started((swap_hbm.at[head], slots[0], sems.at[2]), (down_hbm.at[tail], slots[1], sems.at[3]))

    for copy in first:
        copy.wait()
    for slot in range(2):
        pltpu.make_async_copy(swap_hbm.at[head], slots[slot], sems.at[2 + slot]).wait()

    for r in range(blocks):
        val_copies[r].wait()
        tile_row = jnp.concatenate([vals[r, t] for t in range(tiles)], axis=1)
        picked = jnp.concatenate(
            [ext[pl.ds(pl.multiple_of(cols[r, t] * TILE, TILE), TILE), :] for t in range(tiles)], axis=0
        )
        agg[r * TILE : (r + 1) * TILE, :] = product(tile_row, picked).astype(jnp.bfloat16)
    for copy in later:
        copy.wait()
    chunk = 2 * TILE
    for low in range(0, rows, chunk):
        span = pl.ds(low, chunk)
        preact = product(ext[span, :], w_self[...]) + product(agg[span, :], w_neigh[...])
        sigma = 1.0 / (1.0 + jnp.exp(-preact))
        node_out[span, :] = (preact * sigma).astype(jnp.bfloat16)
        slope = sigma * (1.0 + preact * (1.0 - sigma))
        grad_pre[span, :] = (grad_out[span, :].astype(jnp.float32) * slope).astype(jnp.bfloat16)
    (out_copy,) = started((node_out, node_out_hbm, sems.at[9]))
    parts_ref[0:width, :] = product(ext[0:rows, :], grad_pre[...], 0, 0).astype(jnp.bfloat16)
    parts_ref[width:, :] = product(agg[...], grad_pre[...], 0, 0).astype(jnp.bfloat16)
    out_copy.wait()


def forward(tile_cols, node_feats, swap, up, down, tile_vals, w_self, w_neigh, grad_out):
    rows, width = node_feats.shape
    like = pltpu.VMEM((rows, width), jnp.bfloat16)
    return pl.pallas_call(
        forward_kernel,
        out_shape=[
            jax.ShapeDtypeStruct((rows, width), jnp.bfloat16),
            jax.ShapeDtypeStruct((rows, width), jnp.bfloat16),
            jax.ShapeDtypeStruct((2 * width, width), jnp.bfloat16),
        ],
        in_specs=[HBM, HBM, ANY, ANY, ANY, HBM, HBM, HBM, HBM],
        out_specs=[HBM, VMEM, VMEM],
        scratch_shapes=[
            pltpu.SMEM(tile_cols.shape, jnp.int32),
            pltpu.VMEM((rows + 4 * TILE, width), jnp.bfloat16),
            pltpu.VMEM(tile_vals.shape, jnp.bfloat16),
            like,
            pltpu.VMEM(w_self.shape, jnp.bfloat16),
            pltpu.VMEM(w_neigh.shape, jnp.bfloat16),
            like,
            like,
            pltpu.SemaphoreType.DMA((10,)),
            pltpu.SemaphoreType.DMA((tile_cols.shape[0],)),
        ],
        compiler_params=PARAMS,
        cost_estimate=pl.CostEstimate(flops=1 << 30, bytes_accessed=5 << 20, transcendentals=1 << 18),
        name="forward",
    )(tile_cols, node_feats, swap, up, down, tile_vals, w_self, w_neigh, grad_out)


def backward_kernel(
    cols_hbm, vals_hbm, w_self_hbm, w_neigh_hbm, grad_pre,
    own_ref, swap_ref, up_ref, down_ref,
    cols, vals, w_self, w_neigh, grad_agg, grad_ext, sems, vals_sem,
):
    blocks, tiles = cols.shape
    rows = grad_pre.shape[0]
    first = started(
        (cols_hbm, cols, sems.at[0]), (w_self_hbm, w_self, sems.at[1]), (w_neigh_hbm, w_neigh, sems.at[2])
    )
    val_copies = started(*[(vals_hbm.at[r], vals.at[r], vals_sem.at[r]) for r in range(blocks)])
    for copy in first:
        copy.wait()
    grad_agg[...] = product(grad_pre[...], w_neigh[...], 1, 1).astype(jnp.bfloat16)
    grad_ext[0:rows, :] = product(grad_pre[...], w_self[...], 1, 1)
    grad_ext[rows:, :] = jnp.zeros((4 * TILE, grad_ext.shape[1]), jnp.float32)
    for r in range(blocks):
        val_copies[r].wait()
        tile_row = jnp.concatenate([vals[r, t] for t in range(tiles)], axis=1)
        contrib = product(tile_row, grad_agg[r * TILE : (r + 1) * TILE, :], 0, 0)
        for t in range(tiles):
            place = pl.ds(pl.multiple_of(cols[r, t] * TILE, TILE), TILE)
            grad_ext[place, :] += contrib[t * TILE : (t + 1) * TILE, :]
    own_ref[...] = grad_ext[0:rows, :]
    swap_ref[...] = grad_ext[rows : rows + 2 * TILE, :].astype(jnp.bfloat16)
    down_ref[...] = grad_ext[rows + 2 * TILE : rows + 3 * TILE, :].astype(jnp.bfloat16)
    up_ref[...] = grad_ext[rows + 3 * TILE :, :].astype(jnp.bfloat16)


def backward(tile_cols, tile_vals, w_self, w_neigh, grad_pre):
    rows, width = grad_pre.shape
    return pl.pallas_call(
        backward_kernel,
        out_shape=[jax.ShapeDtypeStruct((rows, width), jnp.float32)]
        + [jax.ShapeDtypeStruct((size, width), jnp.bfloat16) for size in (2 * TILE, TILE, TILE)],
        in_specs=[HBM] * 4 + [VMEM],
        out_specs=[VMEM] * 4,
        scratch_shapes=[
            pltpu.SMEM(tile_cols.shape, jnp.int32),
            pltpu.VMEM(tile_vals.shape, jnp.bfloat16),
            pltpu.VMEM(w_self.shape, jnp.bfloat16),
            pltpu.VMEM(w_neigh.shape, jnp.bfloat16),
            pltpu.VMEM((rows, width), jnp.bfloat16),
            pltpu.VMEM((rows + 4 * TILE, width), jnp.float32),
            pltpu.SemaphoreType.DMA((3,)),
            pltpu.SemaphoreType.DMA((tile_cols.shape[0],)),
        ],
        compiler_params=PARAMS,
        cost_estimate=pl.CostEstimate(flops=1 << 30, bytes_accessed=5 << 20, transcendentals=0),
        name="backward",
    )(tile_cols, tile_vals, w_self, w_neigh, grad_pre)


def collect_kernel(index_hbm, count_hbm, own_ref, swap_ref, up_ref, down_ref, out_ref, index, count, sems):
    rows = own_ref.shape[0]
    for copy in started((index_hbm, index, sems.at[0]), (count_hbm, count, sems.at[1])):
        copy.wait()
    even = lax.axis_index("core") == 0
    returned = [
        jnp.where(even, swap_ref[0:TILE, :], down_ref[TILE:, :]),
        jnp.where(even, up_ref[TILE:, :], swap_ref[TILE:, :]),
        down_ref[0:TILE, :],
        up_ref[0:TILE, :],
    ]
    returned = jnp.concatenate(returned, axis=0)
    listed = [jnp.broadcast_to(listed_rows(index, count, slot), (TILE, TILE)) for slot in range(4)]
    for block in range(rows // TILE):
        span = pl.ds(block * TILE, TILE)
        place = lax.broadcasted_iota(jnp.int32, (TILE, TILE), 0) + block * TILE
        chosen = jnp.concatenate([(row == place).astype(jnp.bfloat16) for row in listed], axis=1)
        out_ref[span, :] = (own_ref[span, :] + product(chosen, returned)).astype(jnp.bfloat16)


def collect(send_index, send_count, own_grad, swap, up, down):
    return pl.pallas_call(
        collect_kernel,
        out_shape=jax.ShapeDtypeStruct(own_grad.shape, jnp.bfloat16),
        in_specs=[HBM] * 2 + [VMEM] * 4,
        out_specs=VMEM,
        scratch_shapes=[
            pltpu.VMEM(send_index.shape, jnp.int32),
            pltpu.SMEM(send_count.shape, jnp.int32),
            pltpu.SemaphoreType.DMA((2,)),
        ],
        compiler_params=PARAMS,
        cost_estimate=pl.CostEstimate(flops=2 * 512 * 1024 * 256, bytes_accessed=2 << 20, transcendentals=0),
        name="collect",
    )(send_index, send_count, own_grad, swap, up, down)


def shards(node_feats, send_index, send_count, tile_cols, tile_vals, w_self, w_neigh, grad_out):
    rows, width = node_feats.shape
    swap, up, down = payloads(send_index, send_count, node_feats)
    swap = swapped(swap)
    up, down = joined(up, down, swap, 0)
    up, down = shifted(up, 2), shifted(down, -2)
    node_out, grad_pre, parts = forward(
        tile_cols, node_feats, swap, up, down, tile_vals, w_self, w_neigh, grad_out
    )

    row_n = lax.axis_size(ROW)
    share = exchange(parts.reshape(row_n, 2 * width // row_n, width), ROW)
    own_grad, swap, up, down = backward(tile_cols, tile_vals, w_self, w_neigh, grad_pre)
    share, swap = lax.optimization_barrier((share, swap))
    swap = swapped(swap)
    up, down = joined(up, down, swap, 1)
    share = share.astype(jnp.float32).sum(0).astype(jnp.bfloat16)
    share = exchange(copies_for(share, "y"), "y").astype(jnp.float32).sum(0)
    share, up, down = lax.optimization_barrier((share, up, down))
    up, down = shifted(up, 2), shifted(down, -2)
    share = exchange(copies_for(share, "z"), "z").sum(0)
    share = (share * float(rows * lax.axis_size(DOM)) ** (-0.5)).astype(jnp.bfloat16)
    share, up, down = lax.optimization_barrier((share, up, down))
    whole = exchange(copies_for(share, ROW), ROW).reshape(2 * width, width)
    grad_nodes = collect(send_index, send_count, own_grad, swap, up, down)
    return (
        node_out,
        grad_nodes,
        whole[:width].astype(jnp.float32),
        whole[width:].astype(jnp.float32),
    )


def solution(mesh):
    grid = Mesh(mesh.devices.reshape(4, 8, 8, 2), DOM)
    placed = (
        P(DOM, None),
        P(DOM, None, None),
        P(DOM, None),
        P(DOM, None),
        P(DOM, None, None, None),
        P(),
        P(),
        P(DOM, None),
    )
    return jax.shard_map(
        shards,
        mesh=grid,
        in_specs=placed,
        out_specs=(P(DOM, None), P(DOM, None), P(), P()),
        check_vma=False,
    )
```

```python
import jax
import jax.numpy as jnp
from jax import lax
from jax.experimental import pallas as pl
from jax.experimental.pallas import tpu as pltpu
from jax.sharding import Mesh, PartitionSpec as P

DOM = ("z", "y", "x", "core")
ROW = ("x", "core")
TILE = 128
PARAMS = pltpu.CompilerParams(vmem_limit_bytes=60 * 1024 * 1024)
VMEM = pl.BlockSpec(memory_space=pltpu.VMEM)
HBM = pl.BlockSpec(memory_space=pltpu.HBM)
ANY = pl.BlockSpec(memory_space=pl.ANY)


def product(left, right, left_dim=1, right_dim=0):
    return lax.dot_general(
        left, right, (((left_dim,), (right_dim,)), ((), ())), preferred_element_type=jnp.float32
    )


def exchange(value, axes):
    return lax.all_to_all(value, axes, 0, 0, tiled=False)


def copies_for(share, axes):
    return jnp.broadcast_to(share, (lax.axis_size(axes),) + share.shape)


def partner(device, swap):
    if swap == 0:
        return device + (1 if device % 2 else -1)
    if swap == 1:
        return device + (2 if device // 2 % 2 else -2)
    return device ^ (2 if swap == 2 else 1)


def swapped(value, swap):
    count = lax.axis_size(DOM)
    pairs = [(device, partner(device, swap)) for device in range(count)]
    return lax.ppermute(value, DOM, [pair for pair in pairs if 0 <= pair[1] < count])


def list_of(swap):
    core, odd = lax.axis_index("core"), lax.axis_index("x") % 2
    return (1 - core, 3 - odd, 2 + odd, core)[swap]


def slot_of(swap):
    core, odd = lax.axis_index("core"), lax.axis_index("x") % 2
    return (core, 2 + odd, 3 - odd, 1 - core)[swap]


def started(*pairs):
    copies = [pltpu.make_async_copy(*pair) for pair in pairs]
    for copy in copies:
        copy.start()
    return copies


def listed_rows(index_ref, count_ref, slot):
    indices = index_ref[0, pl.ds(slot, 1), :]
    lane = lax.broadcasted_iota(jnp.int32, indices.shape, 1)
    return jnp.where(lane < count_ref[0, slot], indices, -1)


def payload_kernel(index_hbm, count_hbm, feats_hbm, *refs):
    outs, (index, count, feats, sems) = refs[:4], refs[4:]
    rows = feats.shape[0]
    index_copy, count_copy, feats_copy = started(
        (index_hbm, index, sems.at[0]), (count_hbm, count, sems.at[1]), (feats_hbm, feats, sems.at[2])
    )
    index_copy.wait()
    count_copy.wait()
    place = lax.broadcasted_iota(jnp.int32, (TILE, TILE), 1)
    chosen = []
    for swap in range(4):
        column = jnp.transpose(jnp.broadcast_to(listed_rows(index, count, list_of(swap)), (TILE, TILE)))
        chosen.append(
            jnp.concatenate(
                [(column == place + block * TILE).astype(jnp.bfloat16) for block in range(rows // TILE)], axis=1
            )
        )
    feats_copy.wait()
    picked = product(jnp.concatenate(chosen, axis=0), feats[...]).astype(jnp.bfloat16)
    for swap in range(4):
        outs[swap][...] = picked[swap * TILE : (swap + 1) * TILE]


def payloads(send_index, send_count, node_feats):
    shape = jax.ShapeDtypeStruct((TILE, node_feats.shape[1]), jnp.bfloat16)
    return pl.pallas_call(
        payload_kernel,
        out_shape=[shape] * 4,
        in_specs=[HBM] * 3,
        out_specs=[VMEM] * 4,
        scratch_shapes=[
            pltpu.VMEM(send_index.shape, jnp.int32),
            pltpu.SMEM(send_count.shape, jnp.int32),
            pltpu.VMEM(node_feats.shape, jnp.bfloat16),
            pltpu.SemaphoreType.DMA((3,)),
        ],
        compiler_params=PARAMS,
        cost_estimate=pl.CostEstimate(flops=2 * 512 * 1024 * 256, bytes_accessed=1 << 20, transcendentals=0),
        name="payload",
    )(send_index, send_count, node_feats)


def forward_kernel(
    cols_hbm, feats_hbm, got0, got1, got2, got3, vals_hbm, w_self_hbm, w_neigh_hbm, grad_out_hbm,
    node_out_hbm, grad_pre_hbm, parts_ref,
    cols, ext, vals, agg, w_self, w_neigh, grad_out, node_out, grad_pre, sems, vals_sem, out_sem,
):
    blocks, tiles = cols.shape
    rows, width = grad_out.shape
    pair = 2 * TILE

    def slot_at(slot):
        return pl.ds(pl.multiple_of(rows + slot * TILE, TILE), TILE)

    first = started(
        (cols_hbm, cols, sems.at[0]),
        (feats_hbm, ext.at[0:rows], sems.at[1]),
        *[(got, ext.at[slot_at(slot_of(k))], sems.at[2 + k]) for k, got in enumerate((got0, got1, got2, got3))],
    )
    val_copies = started(*[(vals_hbm.at[r], vals.at[r], vals_sem.at[r]) for r in range(blocks)])
    later = started(
        (w_self_hbm, w_self, sems.at[6]), (w_neigh_hbm, w_neigh, sems.at[7]), (grad_out_hbm, grad_out, sems.at[8])
    )
    for copy in first:
        copy.wait()
    outs = []
    for r in range(blocks):
        val_copies[r].wait()
        tile_row = jnp.concatenate([vals[r, t] for t in range(tiles)], axis=1)
        picked = jnp.concatenate(
            [ext[pl.ds(pl.multiple_of(cols[r, t] * TILE, TILE), TILE), :] for t in range(tiles)], axis=0
        )
        agg[r * TILE : (r + 1) * TILE, :] = product(tile_row, picked).astype(jnp.bfloat16)
    for copy in later:
        copy.wait()
    for low in range(0, rows, pair):
        span = pl.ds(low, pair)
        preact = product(ext[span, :], w_self[...]) + product(agg[span, :], w_neigh[...])
        sigma = 1.0 / (1.0 + jnp.exp(-preact))
        node_out[span, :] = (preact * sigma).astype(jnp.bfloat16)
        slope = sigma * (1.0 + preact * (1.0 - sigma))
        grad_pre[span, :] = (grad_out[span, :].astype(jnp.float32) * slope).astype(jnp.bfloat16)
        step = low // pair
        outs += started(
            (node_out.at[span], node_out_hbm.at[span], out_sem.at[0, step]),
            (grad_pre.at[span], grad_pre_hbm.at[span], out_sem.at[1, step]),
        )
    parts_ref[0:width, :] = product(ext[0:rows, :], grad_pre[...], 0, 0).astype(jnp.bfloat16)
    parts_ref[width:, :] = product(agg[...], grad_pre[...], 0, 0).astype(jnp.bfloat16)
    for copy in outs:
        copy.wait()


def forward(tile_cols, node_feats, arrived, tile_vals, w_self, w_neigh, grad_out):
    rows, width = node_feats.shape
    like = pltpu.VMEM((rows, width), jnp.bfloat16)
    return pl.pallas_call(
        forward_kernel,
        out_shape=[
            jax.ShapeDtypeStruct((rows, width), jnp.bfloat16),
            jax.ShapeDtypeStruct((rows, width), jnp.bfloat16),
            jax.ShapeDtypeStruct((2 * width, width), jnp.bfloat16),
        ],
        in_specs=[HBM, HBM] + [ANY] * 4 + [HBM] * 4,
        out_specs=[HBM, HBM, VMEM],
        scratch_shapes=[
            pltpu.SMEM(tile_cols.shape, jnp.int32),
            pltpu.VMEM((rows + 4 * TILE, width), jnp.bfloat16),
            pltpu.VMEM(tile_vals.shape, jnp.bfloat16),
            like,
            pltpu.VMEM(w_self.shape, jnp.bfloat16),
            pltpu.VMEM(w_neigh.shape, jnp.bfloat16),
            like,
            like,
            like,
            pltpu.SemaphoreType.DMA((9,)),
            pltpu.SemaphoreType.DMA((tile_cols.shape[0],)),
            pltpu.SemaphoreType.DMA((2, rows // (2 * TILE))),
        ],
        compiler_params=PARAMS,
        cost_estimate=pl.CostEstimate(flops=1 << 30, bytes_accessed=5 << 20, transcendentals=1 << 18),
        name="forward",
    )(tile_cols, node_feats, *arrived, tile_vals, w_self, w_neigh, grad_out)


def backward_kernel(
    cols_hbm, vals_hbm, w_self_hbm, w_neigh_hbm, grad_pre_hbm,
    own_ref, back0, back1, back2, back3,
    cols, vals, w_self, w_neigh, grad_pre, grad_agg, grad_ext, sems, vals_sem,
):
    blocks, tiles = cols.shape
    first = started(
        (grad_pre_hbm, grad_pre, sems.at[0]), (w_neigh_hbm, w_neigh, sems.at[1]), (cols_hbm, cols, sems.at[2])
    )
    val_copies = started(*[(vals_hbm.at[r], vals.at[r], vals_sem.at[r]) for r in range(blocks)])
    (last,) = started((w_self_hbm, w_self, sems.at[3]))
    grad_ext[...] = jnp.zeros_like(grad_ext)
    for copy in first:
        copy.wait()
    grad_agg[...] = product(w_neigh[...], grad_pre[...], 1, 1).astype(jnp.bfloat16)
    for r in range(blocks):
        val_copies[r].wait()
        grad_row = grad_agg[:, r * TILE : (r + 1) * TILE]
        for t in range(tiles):
            grad_ext[cols[r, t]] += product(grad_row, vals[r, t])
    for k, back in enumerate((back0, back1, back2, back3)):
        back[...] = grad_ext[blocks + slot_of(k)].T.astype(jnp.bfloat16)
    last.wait()
    for block in range(blocks):
        span = pl.ds(block * TILE, TILE)
        own_ref[span, :] = product(grad_pre[span, :], w_self[...], 1, 1) + grad_ext[block].T


def backward(tile_cols, tile_vals, w_self, w_neigh, grad_pre):
    rows, width = grad_pre.shape
    return pl.pallas_call(
        backward_kernel,
        out_shape=[jax.ShapeDtypeStruct((rows, width), jnp.float32)]
        + [jax.ShapeDtypeStruct((TILE, width), jnp.bfloat16)] * 4,
        in_specs=[HBM] * 5,
        out_specs=[VMEM] * 5,
        scratch_shapes=[
            pltpu.SMEM(tile_cols.shape, jnp.int32),
            pltpu.VMEM(tile_vals.shape, jnp.bfloat16),
            pltpu.VMEM(w_self.shape, jnp.bfloat16),
            pltpu.VMEM(w_neigh.shape, jnp.bfloat16),
            pltpu.VMEM((rows, width), jnp.bfloat16),
            pltpu.VMEM((width, rows), jnp.bfloat16),
            pltpu.VMEM((rows // TILE + 4, width, TILE), jnp.float32),
            pltpu.SemaphoreType.DMA((4,)),
            pltpu.SemaphoreType.DMA((tile_cols.shape[0],)),
        ],
        compiler_params=PARAMS,
        cost_estimate=pl.CostEstimate(flops=1 << 30, bytes_accessed=5 << 20, transcendentals=0),
        name="backward",
    )(tile_cols, tile_vals, w_self, w_neigh, grad_pre)


def collect_kernel(index_hbm, count_hbm, own_hbm, *refs):
    backs_hbm, (out_hbm, index, count, own, backs, out, sems, out_sem) = refs[:4], refs[4:]
    rows = own.shape[0]
    half = rows // 2
    copies = started(
        (index_hbm, index, sems.at[0]),
        (count_hbm, count, sems.at[1]),
        *[(back, backs.at[k * TILE : (k + 1) * TILE], sems.at[2 + k]) for k, back in enumerate(backs_hbm)],
    )
    own_copies = started(
        *[(own_hbm.at[pl.ds(k * half, half)], own.at[pl.ds(k * half, half)], sems.at[6 + k]) for k in range(2)]
    )
    for copy in copies:
        copy.wait()
    listed = [jnp.broadcast_to(listed_rows(index, count, list_of(k)), (TILE, TILE)) for k in range(4)]
    outs = []
    for k in range(2):
        own_copies[k].wait()
        for block in range(k * half // TILE, (k + 1) * half // TILE):
            span = pl.ds(block * TILE, TILE)
            place = lax.broadcasted_iota(jnp.int32, (TILE, TILE), 0) + block * TILE
            chosen = jnp.concatenate([(row == place).astype(jnp.bfloat16) for row in listed], axis=1)
            out[span, :] = (own[span, :] + product(chosen, backs[...])).astype(jnp.bfloat16)
        outs += started((out.at[pl.ds(k * half, half)], out_hbm.at[pl.ds(k * half, half)], out_sem.at[k]))
    for copy in outs:
        copy.wait()


def collect(send_index, send_count, own_grad, returned):
    rows, width = own_grad.shape
    return pl.pallas_call(
        collect_kernel,
        out_shape=jax.ShapeDtypeStruct((rows, width), jnp.bfloat16),
        in_specs=[HBM] * 3 + [ANY] * 4,
        out_specs=HBM,
        scratch_shapes=[
            pltpu.VMEM(send_index.shape, jnp.int32),
            pltpu.SMEM(send_count.shape, jnp.int32),
            pltpu.VMEM((rows, width), jnp.float32),
            pltpu.VMEM((4 * TILE, width), jnp.bfloat16),
            pltpu.VMEM((rows, width), jnp.bfloat16),
            pltpu.SemaphoreType.DMA((8,)),
            pltpu.SemaphoreType.DMA((2,)),
        ],
        compiler_params=PARAMS,
        cost_estimate=pl.CostEstimate(flops=2 * 512 * 1024 * 256, bytes_accessed=2 << 20, transcendentals=0),
        name="collect",
    )(send_index, send_count, own_grad, *returned)


def shards(node_feats, send_index, send_count, tile_cols, tile_vals, w_self, w_neigh, grad_out):
    rows, width = node_feats.shape
    payload = payloads(send_index, send_count, node_feats)
    arrived = [swapped(payload[swap], swap) for swap in range(4)]
    node_out, grad_pre, parts = forward(
        tile_cols, node_feats, arrived, tile_vals, w_self, w_neigh, grad_out
    )
    row_n = lax.axis_size(ROW)
    share = exchange(parts.reshape(row_n, 2 * width // row_n, width), ROW)
    own_grad, *back = backward(tile_cols, tile_vals, w_self, w_neigh, grad_pre)
    share, *back = lax.optimization_barrier((share, *back))
    returned = [swapped(back[swap], swap) for swap in range(2)]
    share = share.astype(jnp.float32).sum(0).astype(jnp.bfloat16)
    share = exchange(copies_for(share, "y"), "y").astype(jnp.float32).sum(0)
    share, back[2], back[3] = lax.optimization_barrier((share, back[2], back[3]))
    returned += [swapped(back[swap], swap) for swap in range(2, 4)]
    share = exchange(copies_for(share, "z"), "z").sum(0)
    share = (share * float(rows * lax.axis_size(DOM)) ** (-0.5)).astype(jnp.bfloat16)
    share, *returned = lax.optimization_barrier((share, *returned))
    whole = exchange(copies_for(share, ROW), ROW).reshape(2 * width, width)
    grad_nodes = collect(send_index, send_count, own_grad, returned)
    return (
        node_out,
        grad_nodes,
        whole[:width].astype(jnp.float32),
        whole[width:].astype(jnp.float32),
    )


def solution(mesh):
    grid = Mesh(mesh.devices.reshape(4, 8, 8, 2), DOM)
    placed = (
        P(DOM, None),
        P(DOM, None, None),
        P(DOM, None),
        P(DOM, None),
        P(DOM, None, None, None),
        P(),
        P(),
        P(DOM, None),
    )
    return jax.shard_map(
        shards,
        mesh=grid,
        in_specs=placed,
        out_specs=(P(DOM, None), P(DOM, None), P(), P()),
        check_vma=False,
    )
```

```python
import jax
import jax.numpy as jnp
from jax import lax
from jax.experimental import pallas as pl
from jax.experimental.pallas import tpu as pltpu
from jax.sharding import Mesh, PartitionSpec as P

DOM = ("z", "y", "x", "core")
ROW = ("x", "core")
TILE = 128
PARAMS = pltpu.CompilerParams(vmem_limit_bytes=16 * 1024 * 1024)
VMEM = pl.BlockSpec(memory_space=pltpu.VMEM)
HBM = pl.BlockSpec(memory_space=pltpu.HBM)
SMEM = pl.BlockSpec(memory_space=pltpu.SMEM)


def product(left, right, left_dim=1, right_dim=0):
    return lax.dot_general(
        left, right, (((left_dim,), (right_dim,)), ((), ())), preferred_element_type=jnp.float32
    )


def exchange(value, axes):
    return lax.all_to_all(value, axes, 0, 0, tiled=False)


def copies_for(share, axes):
    return jnp.broadcast_to(share, (lax.axis_size(axes),) + share.shape)


def partner(device, swap):
    if swap == 0:
        return device + (1 if device % 2 else -1)
    if swap == 1:
        return device + (2 if device // 2 % 2 else -2)
    return device ^ (2 if swap == 2 else 1)


def swapped(value, swap):
    count = lax.axis_size(DOM)
    pairs = [(device, partner(device, swap)) for device in range(count)]
    return lax.ppermute(value, DOM, [pair for pair in pairs if 0 <= pair[1] < count])


def list_of(swap):
    core, odd = lax.axis_index("core"), lax.axis_index("x") % 2
    return (1 - core, 3 - odd, 2 + odd, core)[swap]


def slot_of(swap):
    core, odd = lax.axis_index("core"), lax.axis_index("x") % 2
    return (core, 2 + odd, 3 - odd, 1 - core)[swap]


def started(*pairs):
    copies = [pltpu.make_async_copy(*pair) for pair in pairs]
    for copy in copies:
        copy.start()
    return copies


def listed_rows(index_ref, count_ref, slot):
    indices = index_ref[0, pl.ds(slot, 1), :]
    lane = lax.broadcasted_iota(jnp.int32, indices.shape, 1)
    return jnp.where(lane < count_ref[0, slot], indices, -1)


def payload_kernel(index_hbm, count_hbm, feats_hbm, *refs):
    outs, (index, count, feats, sems) = refs[:4], refs[4:]
    rows = feats.shape[0]
    index_copy, count_copy, feats_copy = started(
        (index_hbm, index, sems.at[0]), (count_hbm, count, sems.at[1]), (feats_hbm, feats, sems.at[2])
    )
    index_copy.wait()
    count_copy.wait()
    place = lax.broadcasted_iota(jnp.int32, (TILE, TILE), 1)
    chosen = []
    for swap in range(4):
        column = jnp.transpose(jnp.broadcast_to(listed_rows(index, count, list_of(swap)), (TILE, TILE)))
        chosen.append(
            jnp.concatenate(
                [(column == place + block * TILE).astype(jnp.bfloat16) for block in range(rows // TILE)], axis=1
            )
        )
    feats_copy.wait()
    picked = product(jnp.concatenate(chosen, axis=0), feats[...]).astype(jnp.bfloat16)
    for swap in range(4):
        outs[swap][...] = picked[swap * TILE : (swap + 1) * TILE]


def payloads(send_index, send_count, node_feats):
    shape = jax.ShapeDtypeStruct((TILE, node_feats.shape[1]), jnp.bfloat16)
    return pl.pallas_call(
        payload_kernel,
        out_shape=[shape] * 4,
        in_specs=[HBM] * 3,
        out_specs=[VMEM] * 4,
        scratch_shapes=[
            pltpu.VMEM(send_index.shape, jnp.int32),
            pltpu.SMEM(send_count.shape, jnp.int32),
            pltpu.VMEM(node_feats.shape, jnp.bfloat16),
            pltpu.SemaphoreType.DMA((3,)),
        ],
        compiler_params=pltpu.CompilerParams(vmem_limit_bytes=60 * 1024 * 1024),
        cost_estimate=pl.CostEstimate(flops=1 << 36, bytes_accessed=1 << 20, transcendentals=0),
        name="payload",
    )(send_index, send_count, node_feats)


def forward_kernel(
    cols, feats, got0, got1, got2, got3, vals, w_self, w_neigh, grad_out,
    node_out_hbm, grad_pre, parts_ref,
    ext, agg, node_out, out_sem,
):
    blocks, tiles = cols.shape
    rows, width = feats.shape
    pair = 2 * TILE
    ext[0:rows, :] = feats[...]
    for swap, got in enumerate((got0, got1, got2, got3)):
        ext[pl.ds(pl.multiple_of(rows + slot_of(swap) * TILE, TILE), TILE), :] = got[...]
    for r in range(blocks):
        tile_row = jnp.concatenate([vals[r, t] for t in range(tiles)], axis=1)
        picked = jnp.concatenate(
            [ext[pl.ds(pl.multiple_of(cols[r, t] * TILE, TILE), TILE), :] for t in range(tiles)], axis=0
        )
        agg[r * TILE : (r + 1) * TILE, :] = product(tile_row, picked).astype(jnp.bfloat16)
    outs = []
    for low in range(0, rows, pair):
        span = pl.ds(low, pair)
        preact = product(feats[span, :], w_self[...]) + product(agg[span, :], w_neigh[...])
        sigma = 1.0 / (1.0 + jnp.exp(-preact))
        node_out[span, :] = (preact * sigma).astype(jnp.bfloat16)
        slope = sigma * (1.0 + preact * (1.0 - sigma))
        grad_pre[span, :] = (grad_out[span, :].astype(jnp.float32) * slope).astype(jnp.bfloat16)
        outs += started((node_out.at[span], node_out_hbm.at[span], out_sem.at[low // pair]))
    parts_ref[0:width, :] = product(feats[...], grad_pre[...], 0, 0).astype(jnp.bfloat16)
    parts_ref[width:, :] = product(agg[...], grad_pre[...], 0, 0).astype(jnp.bfloat16)
    for copy in outs:
        copy.wait()


def forward(tile_cols, node_feats, arrived, tile_vals, w_self, w_neigh, grad_out):
    rows, width = node_feats.shape
    return pl.pallas_call(
        forward_kernel,
        out_shape=[
            jax.ShapeDtypeStruct((rows, width), jnp.bfloat16),
            jax.ShapeDtypeStruct((rows, width), jnp.bfloat16),
            jax.ShapeDtypeStruct((2 * width, width), jnp.bfloat16),
        ],
        in_specs=[SMEM] + [VMEM] * 9,
        out_specs=[HBM, VMEM, VMEM],
        scratch_shapes=[
            pltpu.VMEM((rows + 4 * TILE, width), jnp.bfloat16),
            pltpu.VMEM((rows, width), jnp.bfloat16),
            pltpu.VMEM((rows, width), jnp.bfloat16),
            pltpu.SemaphoreType.DMA((rows // (2 * TILE),)),
        ],
        compiler_params=PARAMS,
        cost_estimate=pl.CostEstimate(flops=1 << 30, bytes_accessed=5 << 20, transcendentals=1 << 18),
        name="forward",
    )(tile_cols, node_feats, *arrived, tile_vals, w_self, w_neigh, grad_out)


def backward_kernel(
    cols, vals, w_self, w_neigh, grad_pre,
    own_ref, back0, back1, back2, back3,
    grad_agg, grad_ext,
):
    blocks, tiles = cols.shape
    grad_ext[...] = jnp.zeros_like(grad_ext)
    grad_agg[...] = product(w_neigh[...], grad_pre[...], 1, 1).astype(jnp.bfloat16)
    for r in range(blocks):
        grad_row = grad_agg[:, r * TILE : (r + 1) * TILE]
        for t in range(tiles):
            grad_ext[cols[r, t]] += product(grad_row, vals[r, t])
    for swap, back in enumerate((back0, back1, back2, back3)):
        back[...] = grad_ext[blocks + slot_of(swap)].T.astype(jnp.bfloat16)
    for block in range(blocks):
        span = pl.ds(block * TILE, TILE)
        own_ref[span, :] = product(grad_pre[span, :], w_self[...], 1, 1) + grad_ext[block].T


def backward(tile_cols, tile_vals, w_self, w_neigh, grad_pre):
    rows, width = grad_pre.shape
    return pl.pallas_call(
        backward_kernel,
        out_shape=[jax.ShapeDtypeStruct((rows, width), jnp.float32)]
        + [jax.ShapeDtypeStruct((TILE, width), jnp.bfloat16)] * 4,
        in_specs=[SMEM] + [VMEM] * 4,
        out_specs=[VMEM] * 5,
        scratch_shapes=[
            pltpu.VMEM((width, rows), jnp.bfloat16),
            pltpu.VMEM((rows // TILE + 4, width, TILE), jnp.float32),
        ],
        compiler_params=PARAMS,
        cost_estimate=pl.CostEstimate(flops=1 << 30, bytes_accessed=5 << 20, transcendentals=0),
        name="backward",
    )(tile_cols, tile_vals, w_self, w_neigh, grad_pre)


def collect_kernel(index, count, own, back0, back1, back2, back3, out_hbm, out, out_sem):
    rows = own.shape[0]
    pair = 2 * TILE
    returned = jnp.concatenate([back0[...], back1[...], back2[...], back3[...]], axis=0)
    listed = [jnp.broadcast_to(listed_rows(index, count, list_of(swap)), (pair, TILE)) for swap in range(4)]
    outs = []
    for low in range(0, rows, pair):
        span = pl.ds(low, pair)
        place = lax.broadcasted_iota(jnp.int32, (pair, TILE), 0) + low
        chosen = jnp.concatenate([(row == place).astype(jnp.bfloat16) for row in listed], axis=1)
        out[span, :] = (own[span, :] + product(chosen, returned)).astype(jnp.bfloat16)
        outs += started((out.at[span], out_hbm.at[span], out_sem.at[low // pair]))
    for copy in outs:
        copy.wait()


def collect(send_index, send_count, own_grad, returned):
    rows, width = own_grad.shape
    return pl.pallas_call(
        collect_kernel,
        out_shape=jax.ShapeDtypeStruct((rows, width), jnp.bfloat16),
        in_specs=[VMEM, SMEM] + [VMEM] * 5,
        out_specs=HBM,
        scratch_shapes=[
            pltpu.VMEM((rows, width), jnp.bfloat16),
            pltpu.SemaphoreType.DMA((rows // (2 * TILE),)),
        ],
        compiler_params=PARAMS,
        cost_estimate=pl.CostEstimate(flops=2 * 512 * 1024 * 256, bytes_accessed=2 << 20, transcendentals=0),
        name="collect",
    )(send_index, send_count, own_grad, *returned)


def shards(node_feats, send_index, send_count, tile_cols, tile_vals, w_self, w_neigh, grad_out):
    rows, width = node_feats.shape
    payload = payloads(send_index, send_count, node_feats)
    arrived = [swapped(payload[swap], swap) for swap in range(4)]
    node_out, grad_pre, parts = forward(
        tile_cols, node_feats, arrived, tile_vals, w_self, w_neigh, grad_out
    )
    row_n = lax.axis_size(ROW)
    share = exchange(parts.reshape(row_n, 2 * width // row_n, width), ROW)
    own_grad, *back = backward(tile_cols, tile_vals, w_self, w_neigh, grad_pre)
    share = share.astype(jnp.float32).sum(0).astype(jnp.bfloat16)
    share, own_grad, *back = lax.optimization_barrier((share, own_grad, *back))
    share = exchange(copies_for(share, "y"), "y").astype(jnp.float32).sum(0)
    share, *back = lax.optimization_barrier((share, *back))
    returned = [swapped(back[swap], swap) for swap in range(2)]
    share = exchange(copies_for(share, "z"), "z").sum(0)
    share = (share * float(rows * lax.axis_size(DOM)) ** (-0.5)).astype(jnp.bfloat16)
    share, returned[0], returned[1], back[2], back[3] = lax.optimization_barrier(
        (share, returned[0], returned[1], back[2], back[3])
    )
    whole = exchange(copies_for(share, ROW), ROW).reshape(2 * width, width)
    returned += [swapped(back[swap], swap) for swap in range(2, 4)]
    grad_nodes = collect(send_index, send_count, own_grad, returned)
    return (
        node_out,
        grad_nodes,
        whole[:width].astype(jnp.float32),
        whole[width:].astype(jnp.float32),
    )


def solution(mesh):
    grid = Mesh(mesh.devices.reshape(4, 8, 8, 2), DOM)
    placed = (
        P(DOM, None),
        P(DOM, None, None),
        P(DOM, None),
        P(DOM, None),
        P(DOM, None, None, None),
        P(),
        P(),
        P(DOM, None),
    )
    return jax.shard_map(
        shards,
        mesh=grid,
        in_specs=placed,
        out_specs=(P(DOM, None), P(DOM, None), P(), P()),
        check_vma=False,
    )
```

```python
import jax
import jax.numpy as jnp
from jax import lax
from jax.experimental import pallas as pl
from jax.experimental.pallas import tpu as pltpu
from jax.sharding import Mesh, PartitionSpec as P

DOM = ("z", "y", "x", "core")
ROW = ("x", "core")
TILE = 128
PARAMS = pltpu.CompilerParams(vmem_limit_bytes=16 * 1024 * 1024)
VMEM = pl.BlockSpec(memory_space=pltpu.VMEM)
HBM = pl.BlockSpec(memory_space=pltpu.HBM)
SMEM = pl.BlockSpec(memory_space=pltpu.SMEM)


def product(left, right, left_dim=1, right_dim=0):
    return lax.dot_general(
        left, right, (((left_dim,), (right_dim,)), ((), ())), preferred_element_type=jnp.float32
    )


def ahead(values):
    return lax.optimization_barrier(values)


def exchange(value, axes):
    return lax.all_to_all(value, axes, 0, 0, tiled=False)


def copies_for(share, axes):
    return jnp.broadcast_to(share, (lax.axis_size(axes),) + share.shape)


def partner(device, swap):
    if swap == 0:
        return device + (1 if device % 2 else -1)
    if swap == 1:
        return device + (2 if device // 2 % 2 else -2)
    return device ^ (2 if swap == 2 else 1)


def swapped(value, swap):
    count = lax.axis_size(DOM)
    pairs = [(device, partner(device, swap)) for device in range(count)]
    return lax.ppermute(value, DOM, [pair for pair in pairs if 0 <= pair[1] < count])


def list_of(swap):
    core, odd = lax.axis_index("core"), lax.axis_index("x") % 2
    return (1 - core, 3 - odd, 2 + odd, core)[swap]


def slot_of(swap):
    core, odd = lax.axis_index("core"), lax.axis_index("x") % 2
    return (core, 2 + odd, 3 - odd, 1 - core)[swap]


def started(*pairs):
    copies = [pltpu.make_async_copy(*pair) for pair in pairs]
    for copy in copies:
        copy.start()
    return copies


def listed_rows(index_ref, count_ref, slot):
    indices = index_ref[0, pl.ds(slot, 1), :]
    lane = lax.broadcasted_iota(jnp.int32, indices.shape, 1)
    return jnp.where(lane < count_ref[0, slot], indices, -1)


def payload_kernel(index_hbm, count_hbm, feats_hbm, *refs):
    outs, (index, count, feats, picked, sems, out_sem) = refs[:4], refs[4:]
    rows = feats.shape[0]
    index_copy, count_copy, feats_copy = started(
        (index_hbm, index, sems.at[0]), (count_hbm, count, sems.at[1]), (feats_hbm, feats, sems.at[2])
    )
    index_copy.wait()
    count_copy.wait()
    place = lax.broadcasted_iota(jnp.int32, (TILE, TILE), 1)
    chosen = []
    for swap in range(4):
        column = jnp.transpose(jnp.broadcast_to(listed_rows(index, count, list_of(swap)), (TILE, TILE)))
        chosen.append(
            jnp.concatenate(
                [(column == place + block * TILE).astype(jnp.bfloat16) for block in range(rows // TILE)], axis=1
            )
        )
    feats_copy.wait()
    copies = []
    for swap in range(4):
        picked[swap] = product(chosen[swap], feats[...]).astype(jnp.bfloat16)
        copies += started((picked.at[swap], outs[swap], out_sem.at[swap]))
    for copy in copies:
        copy.wait()


def payloads(send_index, send_count, node_feats):
    shape = jax.ShapeDtypeStruct((TILE, node_feats.shape[1]), jnp.bfloat16)
    return pl.pallas_call(
        payload_kernel,
        out_shape=[shape] * 4,
        in_specs=[HBM] * 3,
        out_specs=[HBM] * 4,
        scratch_shapes=[
            pltpu.VMEM(send_index.shape, jnp.int32),
            pltpu.SMEM(send_count.shape, jnp.int32),
            pltpu.VMEM(node_feats.shape, jnp.bfloat16),
            pltpu.VMEM((4, *shape.shape), jnp.bfloat16),
            pltpu.SemaphoreType.DMA((3,)),
            pltpu.SemaphoreType.DMA((4,)),
        ],
        compiler_params=pltpu.CompilerParams(vmem_limit_bytes=60 * 1024 * 1024),
        cost_estimate=pl.CostEstimate(flops=1 << 36, bytes_accessed=1 << 20, transcendentals=0),
        name="payload",
    )(send_index, send_count, node_feats)


def layer_kernel(
    cols, feats, got0, got1, got2, got3, vals, w_self, w_neigh, grad_out,
    node_out_hbm, parts_ref, own_ref, near_ref, far_ref, pair_ref,
    ext, agg, node_out, grad_pre, grad_agg, grad_ext, out_sem,
):
    blocks, tiles = cols.shape
    rows, width = feats.shape
    pair = 2 * TILE
    ext[0:rows, :] = feats[...]
    for swap, got in enumerate((got0, got1, got2, got3)):
        ext[pl.ds(pl.multiple_of(rows + slot_of(swap) * TILE, TILE), TILE), :] = got[...]
    grad_ext[...] = jnp.zeros_like(grad_ext)
    for r in range(blocks):
        tile_row = jnp.concatenate([vals[r, t] for t in range(tiles)], axis=1)
        picked = jnp.concatenate(
            [ext[pl.ds(pl.multiple_of(cols[r, t] * TILE, TILE), TILE), :] for t in range(tiles)], axis=0
        )
        agg[r * TILE : (r + 1) * TILE, :] = product(tile_row, picked).astype(jnp.bfloat16)
    outs = []
    for low in range(0, rows, pair):
        span = pl.ds(low, pair)
        preact = product(feats[span, :], w_self[...]) + product(agg[span, :], w_neigh[...])
        sigma = 1.0 / (1.0 + jnp.exp(-preact))
        node_out[span, :] = (preact * sigma).astype(jnp.bfloat16)
        slope = sigma * (1.0 + preact * (1.0 - sigma))
        grad_pre[span, :] = (grad_out[span, :].astype(jnp.float32) * slope).astype(jnp.bfloat16)
        outs += started((node_out.at[span], node_out_hbm.at[span], out_sem.at[low // pair]))
    grad_agg[...] = product(w_neigh[...], grad_pre[...], 1, 1).astype(jnp.bfloat16)
    parts_ref[0:width, :] = product(feats[...], grad_pre[...], 0, 0).astype(jnp.bfloat16)
    parts_ref[width:, :] = product(agg[...], grad_pre[...], 0, 0).astype(jnp.bfloat16)
    for r in range(blocks):
        grad_row = grad_agg[:, r * TILE : (r + 1) * TILE]
        for t in range(tiles):
            grad_ext[cols[r, t]] += product(grad_row, vals[r, t])
    for slot in range(2):
        near_ref[slot * TILE : (slot + 1) * TILE, :] = grad_ext[blocks + slot].T.astype(jnp.bfloat16)
    far_ref[...] = grad_ext[blocks + slot_of(1)].T.astype(jnp.bfloat16)
    pair_ref[...] = grad_ext[blocks + slot_of(2)].T.astype(jnp.bfloat16)
    for block in range(blocks):
        span = pl.ds(block * TILE, TILE)
        own_ref[span, :] = product(grad_pre[span, :], w_self[...], 1, 1) + grad_ext[block].T
    for copy in outs:
        copy.wait()


def layer(tile_cols, node_feats, arrived, tile_vals, w_self, w_neigh, grad_out):
    rows, width = node_feats.shape
    like = pltpu.VMEM((rows, width), jnp.bfloat16)
    return pl.pallas_call(
        layer_kernel,
        out_shape=[
            jax.ShapeDtypeStruct((rows, width), jnp.bfloat16),
            jax.ShapeDtypeStruct((2 * width, width), jnp.bfloat16),
            jax.ShapeDtypeStruct((rows, width), jnp.float32),
        ]
        + [jax.ShapeDtypeStruct((size, width), jnp.bfloat16) for size in (2 * TILE, TILE, TILE)],
        in_specs=[SMEM] + [VMEM] * 9,
        out_specs=[HBM] + [VMEM] * 5,
        scratch_shapes=[
            pltpu.VMEM((rows + 4 * TILE, width), jnp.bfloat16),
            like,
            like,
            like,
            pltpu.VMEM((width, rows), jnp.bfloat16),
            pltpu.VMEM((rows // TILE + 4, width, TILE), jnp.float32),
            pltpu.SemaphoreType.DMA((rows // (2 * TILE),)),
        ],
        compiler_params=PARAMS,
        cost_estimate=pl.CostEstimate(flops=2 << 30, bytes_accessed=5 << 20, transcendentals=1 << 18),
        name="layer",
    )(tile_cols, node_feats, *arrived, tile_vals, w_self, w_neigh, grad_out)


def join_kernel(near_ref, far_ref, pair_ref, far_out, pair_out):
    odd = lax.axis_index("x") % 2
    for out, ref, half in ((far_out, far_ref, odd), (pair_out, pair_ref, 1 - odd)):
        out[0:TILE, :] = ref[...]
        out[TILE:, :] = near_ref[pl.ds(pl.multiple_of(half * TILE, TILE), TILE), :]


def joined(near, far, pair):
    return pl.pallas_call(
        join_kernel,
        out_shape=[jax.ShapeDtypeStruct(near.shape, near.dtype)] * 2,
        in_specs=[VMEM] * 3,
        out_specs=[VMEM] * 2,
        compiler_params=pltpu.CompilerParams(vmem_limit_bytes=4 * 1024 * 1024),
        name="join",
    )(near, far, pair)


def collect_kernel(index, count, own, near, far, pair_rows, out_hbm, out, out_sem):
    rows = own.shape[0]
    pair = 2 * TILE
    core, odd = lax.axis_index("core"), lax.axis_index("x") % 2
    passed = jnp.where(core == odd, far[TILE:, :], pair_rows[TILE:, :])
    swapped_rows = near[pl.ds(pl.multiple_of(core * TILE, TILE), TILE), :]
    returned = jnp.concatenate([passed, far[0:TILE, :], pair_rows[0:TILE, :], swapped_rows], axis=0)
    listed = [jnp.broadcast_to(listed_rows(index, count, list_of(swap)), (pair, TILE)) for swap in range(4)]
    outs = []
    for low in range(0, rows, pair):
        span = pl.ds(low, pair)
        place = lax.broadcasted_iota(jnp.int32, (pair, TILE), 0) + low
        chosen = jnp.concatenate([(row == place).astype(jnp.bfloat16) for row in listed], axis=1)
        out[span, :] = (own[span, :] + product(chosen, returned)).astype(jnp.bfloat16)
        outs += started((out.at[span], out_hbm.at[span], out_sem.at[low // pair]))
    for copy in outs:
        copy.wait()


def collect(send_index, send_count, own_grad, near, far, pair):
    rows, width = own_grad.shape
    return pl.pallas_call(
        collect_kernel,
        out_shape=jax.ShapeDtypeStruct((rows, width), jnp.bfloat16),
        in_specs=[VMEM, SMEM] + [VMEM] * 4,
        out_specs=HBM,
        scratch_shapes=[
            pltpu.VMEM((rows, width), jnp.bfloat16),
            pltpu.SemaphoreType.DMA((rows // (2 * TILE),)),
        ],
        compiler_params=PARAMS,
        cost_estimate=pl.CostEstimate(flops=2 * 512 * 1024 * 256, bytes_accessed=2 << 20, transcendentals=0),
        name="collect",
    )(send_index, send_count, own_grad, near, far, pair)


def shards(node_feats, send_index, send_count, tile_cols, tile_vals, w_self, w_neigh, grad_out):
    rows, width = node_feats.shape
    payload = payloads(send_index, send_count, node_feats)
    arrived = [swapped(payload[swap], swap) for swap in range(4)]
    node_out, parts, own_grad, near, far, pair = layer(
        tile_cols, node_feats, arrived, tile_vals, w_self, w_neigh, grad_out
    )
    row_n = lax.axis_size(ROW)
    share = exchange(parts.reshape(row_n, 2 * width // row_n, width), ROW)
    near = swapped(near, 3)
    far, pair = joined(near, far, pair)
    pair = swapped(pair, 2)
    share, near, far, pair = ahead((share, near, far, pair))
    share = share.astype(jnp.float32).sum(0).astype(jnp.bfloat16)
    share = exchange(copies_for(share, "y"), "y").astype(jnp.float32).sum(0)
    share = exchange(copies_for(share, "z"), "z").sum(0)
    share = (share * float(rows * lax.axis_size(DOM)) ** (-0.5)).astype(jnp.bfloat16)
    share, far = ahead((share, far))
    whole = exchange(copies_for(share, ROW), ROW).reshape(2 * width, width)
    far = swapped(far, 1)
    grad_nodes = collect(send_index, send_count, own_grad, near, far, pair)
    return (
        node_out,
        grad_nodes,
        whole[:width].astype(jnp.float32),
        whole[width:].astype(jnp.float32),
    )


def solution(mesh):
    grid = Mesh(mesh.devices.reshape(4, 8, 8, 2), DOM)
    placed = (
        P(DOM, None),
        P(DOM, None, None),
        P(DOM, None),
        P(DOM, None),
        P(DOM, None, None, None),
        P(),
        P(),
        P(DOM, None),
    )
    return jax.shard_map(
        shards,
        mesh=grid,
        in_specs=placed,
        out_specs=(P(DOM, None), P(DOM, None), P(), P()),
        check_vma=False,
    )
```

```python
import jax
import jax.numpy as jnp
from jax import lax
from jax.experimental import pallas as pl
from jax.experimental.pallas import tpu as pltpu
from jax.sharding import Mesh, PartitionSpec as P

DOM = ("z", "y", "x", "core")
ROW = ("x", "core")
TILE = 128
PARAMS = pltpu.CompilerParams(vmem_limit_bytes=16 * 1024 * 1024)
VMEM = pl.BlockSpec(memory_space=pltpu.VMEM)
HBM = pl.BlockSpec(memory_space=pltpu.HBM)
SMEM = pl.BlockSpec(memory_space=pltpu.SMEM)


def product(left, right, left_dim=1, right_dim=0):
    return lax.dot_general(
        left, right, (((left_dim,), (right_dim,)), ((), ())), preferred_element_type=jnp.float32
    )


def ahead(values):
    return lax.optimization_barrier(values)


def exchange(value, axes):
    return lax.all_to_all(value, axes, 0, 0, tiled=False)


def copies_for(share, axes):
    return jnp.broadcast_to(share, (lax.axis_size(axes),) + share.shape)


def partner(device, swap):
    if swap == 0:
        return device + (1 if device % 2 else -1)
    if swap == 1:
        return device + (2 if device // 2 % 2 else -2)
    return device ^ (2 if swap == 2 else 1)


def swapped(value, swap):
    count = lax.axis_size(DOM)
    pairs = [(device, partner(device, swap)) for device in range(count)]
    return lax.ppermute(value, DOM, [pair for pair in pairs if 0 <= pair[1] < count])


def list_of(swap):
    core, odd = lax.axis_index("core"), lax.axis_index("x") % 2
    return (1 - core, 3 - odd, 2 + odd, core)[swap]


def slot_of(swap):
    core, odd = lax.axis_index("core"), lax.axis_index("x") % 2
    return (core, 2 + odd, 3 - odd, 1 - core)[swap]


def started(*pairs):
    copies = [pltpu.make_async_copy(*pair) for pair in pairs]
    for copy in copies:
        copy.start()
    return copies


def listed_rows(index_ref, count_ref, slot):
    indices = index_ref[0, pl.ds(slot, 1), :]
    lane = lax.broadcasted_iota(jnp.int32, indices.shape, 1)
    return jnp.where(lane < count_ref[0, slot], indices, -1)


def payload_kernel(index_hbm, count_hbm, feats_hbm, *refs):
    outs, (index, count, feats, sems) = refs[:4], refs[4:]
    rows = feats.shape[0]
    index_copy, count_copy, feats_copy = started(
        (index_hbm, index, sems.at[0]), (count_hbm, count, sems.at[1]), (feats_hbm, feats, sems.at[2])
    )
    index_copy.wait()
    count_copy.wait()
    place = lax.broadcasted_iota(jnp.int32, (TILE, TILE), 1)
    chosen = []
    for swap in range(4):
        column = jnp.transpose(jnp.broadcast_to(listed_rows(index, count, list_of(swap)), (TILE, TILE)))
        chosen.append(
            jnp.concatenate(
                [(column == place + block * TILE).astype(jnp.bfloat16) for block in range(rows // TILE)], axis=1
            )
        )
    feats_copy.wait()
    picked = product(jnp.concatenate(chosen, axis=0), feats[...]).astype(jnp.bfloat16)
    for swap in range(4):
        outs[swap][...] = picked[swap * TILE : (swap + 1) * TILE]


def payloads(send_index, send_count, node_feats):
    shape = jax.ShapeDtypeStruct((TILE, node_feats.shape[1]), jnp.bfloat16)
    return pl.pallas_call(
        payload_kernel,
        out_shape=[shape] * 4,
        in_specs=[HBM] * 3,
        out_specs=[VMEM] * 4,
        scratch_shapes=[
            pltpu.VMEM(send_index.shape, jnp.int32),
            pltpu.SMEM(send_count.shape, jnp.int32),
            pltpu.VMEM(node_feats.shape, jnp.bfloat16),
            pltpu.SemaphoreType.DMA((3,)),
        ],
        compiler_params=pltpu.CompilerParams(vmem_limit_bytes=60 * 1024 * 1024),
        cost_estimate=pl.CostEstimate(flops=1 << 36, bytes_accessed=1 << 20, transcendentals=0),
        name="payload",
    )(send_index, send_count, node_feats)


def forward_kernel(
    cols, feats, got0, got1, got2, got3, vals, w_self, w_neigh, grad_out,
    node_out_hbm, grad_pre, parts_ref,
    ext, agg, node_out, out_sem,
):
    blocks, tiles = cols.shape
    rows, width = feats.shape
    pair = 2 * TILE
    ext[0:rows, :] = feats[...]
    for swap, got in enumerate((got0, got1, got2, got3)):
        ext[pl.ds(pl.multiple_of(rows + slot_of(swap) * TILE, TILE), TILE), :] = got[...]
    for r in range(blocks):
        tile_row = jnp.concatenate([vals[r, t] for t in range(tiles)], axis=1)
        picked = jnp.concatenate(
            [ext[pl.ds(pl.multiple_of(cols[r, t] * TILE, TILE), TILE), :] for t in range(tiles)], axis=0
        )
        agg[r * TILE : (r + 1) * TILE, :] = product(tile_row, picked).astype(jnp.bfloat16)
    outs = []
    for low in range(0, rows, pair):
        span = pl.ds(low, pair)
        preact = product(feats[span, :], w_self[...]) + product(agg[span, :], w_neigh[...])
        sigma = 1.0 / (1.0 + jnp.exp(-preact))
        node_out[span, :] = (preact * sigma).astype(jnp.bfloat16)
        slope = sigma * (1.0 + preact * (1.0 - sigma))
        grad_pre[span, :] = (grad_out[span, :].astype(jnp.float32) * slope).astype(jnp.bfloat16)
        outs += started((node_out.at[span], node_out_hbm.at[span], out_sem.at[low // pair]))
    parts_ref[0:width, :] = product(feats[...], grad_pre[...], 0, 0).astype(jnp.bfloat16)
    parts_ref[width:, :] = product(agg[...], grad_pre[...], 0, 0).astype(jnp.bfloat16)
    for copy in outs:
        copy.wait()


def forward(tile_cols, node_feats, arrived, tile_vals, w_self, w_neigh, grad_out):
    rows, width = node_feats.shape
    return pl.pallas_call(
        forward_kernel,
        out_shape=[
            jax.ShapeDtypeStruct((rows, width), jnp.bfloat16),
            jax.ShapeDtypeStruct((rows, width), jnp.bfloat16),
            jax.ShapeDtypeStruct((2 * width, width), jnp.bfloat16),
        ],
        in_specs=[SMEM] + [VMEM] * 9,
        out_specs=[HBM, VMEM, VMEM],
        scratch_shapes=[
            pltpu.VMEM((rows + 4 * TILE, width), jnp.bfloat16),
            pltpu.VMEM((rows, width), jnp.bfloat16),
            pltpu.VMEM((rows, width), jnp.bfloat16),
            pltpu.SemaphoreType.DMA((rows // (2 * TILE),)),
        ],
        compiler_params=PARAMS,
        cost_estimate=pl.CostEstimate(flops=1 << 30, bytes_accessed=5 << 20, transcendentals=1 << 18),
        name="forward",
    )(tile_cols, node_feats, *arrived, tile_vals, w_self, w_neigh, grad_out)


def backward_kernel(
    cols, vals, w_self, w_neigh, grad_pre,
    own_ref, back0, back1, back2, back3,
    grad_agg, grad_ext,
):
    blocks, tiles = cols.shape
    grad_ext[...] = jnp.zeros_like(grad_ext)
    grad_agg[...] = product(w_neigh[...], grad_pre[...], 1, 1).astype(jnp.bfloat16)
    for r in range(blocks):
        grad_row = grad_agg[:, r * TILE : (r + 1) * TILE]
        for t in range(tiles):
            grad_ext[cols[r, t]] += product(grad_row, vals[r, t])
    for swap, back in enumerate((back0, back1, back2, back3)):
        back[...] = grad_ext[blocks + slot_of(swap)].T.astype(jnp.bfloat16)
    for block in range(blocks):
        span = pl.ds(block * TILE, TILE)
        own_ref[span, :] = product(grad_pre[span, :], w_self[...], 1, 1) + grad_ext[block].T


def backward(tile_cols, tile_vals, w_self, w_neigh, grad_pre):
    rows, width = grad_pre.shape
    return pl.pallas_call(
        backward_kernel,
        out_shape=[jax.ShapeDtypeStruct((rows, width), jnp.float32)]
        + [jax.ShapeDtypeStruct((TILE, width), jnp.bfloat16)] * 4,
        in_specs=[SMEM] + [VMEM] * 4,
        out_specs=[VMEM] * 5,
        scratch_shapes=[
            pltpu.VMEM((width, rows), jnp.bfloat16),
            pltpu.VMEM((rows // TILE + 4, width, TILE), jnp.float32),
        ],
        compiler_params=PARAMS,
        cost_estimate=pl.CostEstimate(flops=1 << 30, bytes_accessed=5 << 20, transcendentals=0),
        name="backward",
    )(tile_cols, tile_vals, w_self, w_neigh, grad_pre)


def collect_kernel(index, count, own, back0, back1, back2, back3, out_hbm, out, out_sem):
    rows = own.shape[0]
    pair = 2 * TILE
    returned = jnp.concatenate([back0[...], back1[...], back2[...], back3[...]], axis=0)
    listed = [jnp.broadcast_to(listed_rows(index, count, list_of(swap)), (pair, TILE)) for swap in range(4)]
    outs = []
    for low in range(0, rows, pair):
        span = pl.ds(low, pair)
        place = lax.broadcasted_iota(jnp.int32, (pair, TILE), 0) + low
        chosen = jnp.concatenate([(row == place).astype(jnp.bfloat16) for row in listed], axis=1)
        out[span, :] = (own[span, :] + product(chosen, returned)).astype(jnp.bfloat16)
        outs += started((out.at[span], out_hbm.at[span], out_sem.at[low // pair]))
    for copy in outs:
        copy.wait()


def collect(send_index, send_count, own_grad, returned):
    rows, width = own_grad.shape
    return pl.pallas_call(
        collect_kernel,
        out_shape=jax.ShapeDtypeStruct((rows, width), jnp.bfloat16),
        in_specs=[VMEM, SMEM] + [VMEM] * 5,
        out_specs=HBM,
        scratch_shapes=[
            pltpu.VMEM((rows, width), jnp.bfloat16),
            pltpu.SemaphoreType.DMA((rows // (2 * TILE),)),
        ],
        compiler_params=PARAMS,
        cost_estimate=pl.CostEstimate(flops=2 * 512 * 1024 * 256, bytes_accessed=2 << 20, transcendentals=0),
        name="collect",
    )(send_index, send_count, own_grad, *returned)


def shards(node_feats, send_index, send_count, tile_cols, tile_vals, w_self, w_neigh, grad_out):
    rows, width = node_feats.shape
    payload = payloads(send_index, send_count, node_feats)
    arrived = [swapped(payload[swap], swap) for swap in range(4)]
    node_out, grad_pre, parts = forward(
        tile_cols, node_feats, arrived, tile_vals, w_self, w_neigh, grad_out
    )
    row_n = lax.axis_size(ROW)
    share = exchange(parts.reshape(row_n, 2 * width // row_n, width), ROW)
    own_grad, *back = backward(tile_cols, tile_vals, w_self, w_neigh, grad_pre)
    returned = [None] * 4
    returned[3] = swapped(back[3], 3)
    share, own_grad, returned[3], *back = ahead((share, own_grad, returned[3], *back))
    returned[0] = swapped(back[0], 0)
    share = share.astype(jnp.float32).sum(0).astype(jnp.bfloat16)
    share = exchange(copies_for(share, "y"), "y").astype(jnp.float32).sum(0)
    share, returned[0], back[1], back[2] = ahead((share, returned[0], back[1], back[2]))
    share = exchange(copies_for(share, "z"), "z").sum(0)
    share = (share * float(rows * lax.axis_size(DOM)) ** (-0.5)).astype(jnp.bfloat16)
    share, back[1], back[2] = ahead((share, back[1], back[2]))
    whole = exchange(copies_for(share, ROW), ROW).reshape(2 * width, width)
    returned[1], returned[2] = swapped(back[1], 1), swapped(back[2], 2)
    grad_nodes = collect(send_index, send_count, own_grad, returned)
    return (
        node_out,
        grad_nodes,
        whole[:width].astype(jnp.float32),
        whole[width:].astype(jnp.float32),
    )


def solution(mesh):
    grid = Mesh(mesh.devices.reshape(4, 8, 8, 2), DOM)
    placed = (
        P(DOM, None),
        P(DOM, None, None),
        P(DOM, None),
        P(DOM, None),
        P(DOM, None, None, None),
        P(),
        P(),
        P(DOM, None),
    )
    return jax.shard_map(
        shards,
        mesh=grid,
        in_specs=placed,
        out_specs=(P(DOM, None), P(DOM, None), P(), P()),
        check_vma=False,
    )
```

```python
import jax
import jax.numpy as jnp
from jax import lax
from jax.experimental import pallas as pl
from jax.experimental.pallas import tpu as pltpu
from jax.sharding import Mesh, PartitionSpec as P

DOM = ("z", "y", "x", "core")
ROW = ("x", "core")
TILE = 128
PARAMS = pltpu.CompilerParams(vmem_limit_bytes=16 * 1024 * 1024)
VMEM = pl.BlockSpec(memory_space=pltpu.VMEM)
HBM = pl.BlockSpec(memory_space=pltpu.HBM)
SMEM = pl.BlockSpec(memory_space=pltpu.SMEM)


def product(left, right, left_dim=1, right_dim=0):
    return lax.dot_general(
        left, right, (((left_dim,), (right_dim,)), ((), ())), preferred_element_type=jnp.float32
    )


def ahead(values):
    return lax.optimization_barrier(values)


def exchange(value, axes):
    return lax.all_to_all(value, axes, 0, 0, tiled=False)


def copies_for(share, axes):
    return jnp.broadcast_to(share, (lax.axis_size(axes),) + share.shape)


def partner(device, swap):
    if swap == 0:
        return device + (1 if device % 2 else -1)
    if swap == 1:
        return device + (2 if device // 2 % 2 else -2)
    return device ^ (2 if swap == 2 else 1)


def swapped(value, swap):
    count = lax.axis_size(DOM)
    pairs = [(device, partner(device, swap)) for device in range(count)]
    return lax.ppermute(value, DOM, [pair for pair in pairs if 0 <= pair[1] < count])


def list_of(swap):
    core, odd = lax.axis_index("core"), lax.axis_index("x") % 2
    return (1 - core, 3 - odd, 2 + odd, core)[swap]


def slot_of(swap):
    core, odd = lax.axis_index("core"), lax.axis_index("x") % 2
    return (core, 2 + odd, 3 - odd, 1 - core)[swap]


def started(*pairs):
    copies = [pltpu.make_async_copy(*pair) for pair in pairs]
    for copy in copies:
        copy.start()
    return copies


def listed_rows(index_ref, count_ref, slot):
    indices = index_ref[0, pl.ds(slot, 1), :]
    lane = lax.broadcasted_iota(jnp.int32, indices.shape, 1)
    return jnp.where(lane < count_ref[0, slot], indices, -1)


def payload_kernel(index_hbm, count_hbm, feats_hbm, *refs):
    outs, (index, count, feats, sems) = refs[:4], refs[4:]
    rows = feats.shape[0]
    index_copy, count_copy, feats_copy = started(
        (index_hbm, index, sems.at[0]), (count_hbm, count, sems.at[1]), (feats_hbm, feats, sems.at[2])
    )
    index_copy.wait()
    count_copy.wait()
    place = lax.broadcasted_iota(jnp.int32, (TILE, TILE), 1)
    chosen = []
    for swap in range(4):
        column = jnp.transpose(jnp.broadcast_to(listed_rows(index, count, list_of(swap)), (TILE, TILE)))
        chosen.append(
            jnp.concatenate(
                [(column == place + block * TILE).astype(jnp.bfloat16) for block in range(rows // TILE)], axis=1
            )
        )
    feats_copy.wait()
    picked = product(jnp.concatenate(chosen, axis=0), feats[...]).astype(jnp.bfloat16)
    for swap in range(4):
        outs[swap][...] = picked[swap * TILE : (swap + 1) * TILE]


def payloads(send_index, send_count, node_feats):
    shape = jax.ShapeDtypeStruct((TILE, node_feats.shape[1]), jnp.bfloat16)
    return pl.pallas_call(
        payload_kernel,
        out_shape=[shape] * 4,
        in_specs=[HBM] * 3,
        out_specs=[VMEM] * 4,
        scratch_shapes=[
            pltpu.VMEM(send_index.shape, jnp.int32),
            pltpu.SMEM(send_count.shape, jnp.int32),
            pltpu.VMEM(node_feats.shape, jnp.bfloat16),
            pltpu.SemaphoreType.DMA((3,)),
        ],
        compiler_params=pltpu.CompilerParams(vmem_limit_bytes=58 * 1024 * 1024),
        cost_estimate=pl.CostEstimate(flops=1 << 36, bytes_accessed=1 << 20, transcendentals=0),
        name="payload",
    )(send_index, send_count, node_feats)


def layer_kernel(
    cols, feats, got0, got1, got2, got3, vals, w_self, w_neigh, grad_out,
    node_out_hbm, parts_ref, own_ref, back0, back1, back2, back3,
    ext, agg, node_out, grad_pre, grad_agg, grad_ext, out_sem,
):
    blocks, tiles = cols.shape
    rows, width = feats.shape
    pair = 2 * TILE
    ext[0:rows, :] = feats[...]
    for swap, got in enumerate((got0, got1, got2, got3)):
        ext[pl.ds(pl.multiple_of(rows + slot_of(swap) * TILE, TILE), TILE), :] = got[...]
    grad_ext[...] = jnp.zeros_like(grad_ext)
    for r in range(blocks):
        tile_row = jnp.concatenate([vals[r, t] for t in range(tiles)], axis=1)
        picked = jnp.concatenate(
            [ext[pl.ds(pl.multiple_of(cols[r, t] * TILE, TILE), TILE), :] for t in range(tiles)], axis=0
        )
        agg[r * TILE : (r + 1) * TILE, :] = product(tile_row, picked).astype(jnp.bfloat16)
    outs = []
    for low in range(0, rows, pair):
        span = pl.ds(low, pair)
        preact = product(feats[span, :], w_self[...]) + product(agg[span, :], w_neigh[...])
        sigma = 1.0 / (1.0 + jnp.exp(-preact))
        node_out[span, :] = (preact * sigma).astype(jnp.bfloat16)
        slope = sigma * (1.0 + preact * (1.0 - sigma))
        grad_pre[span, :] = (grad_out[span, :].astype(jnp.float32) * slope).astype(jnp.bfloat16)
        outs += started((node_out.at[span], node_out_hbm.at[span], out_sem.at[low // pair]))
    grad_agg[...] = product(w_neigh[...], grad_pre[...], 1, 1).astype(jnp.bfloat16)
    parts_ref[0:width, :] = product(feats[...], grad_pre[...], 0, 0).astype(jnp.bfloat16)
    parts_ref[width:, :] = product(agg[...], grad_pre[...], 0, 0).astype(jnp.bfloat16)
    for r in range(blocks):
        grad_row = grad_agg[:, r * TILE : (r + 1) * TILE]
        for t in range(tiles):
            grad_ext[cols[r, t]] += product(grad_row, vals[r, t])
    for swap, back in enumerate((back0, back1, back2, back3)):
        back[...] = grad_ext[blocks + slot_of(swap)].T.astype(jnp.bfloat16)
    for block in range(blocks):
        span = pl.ds(block * TILE, TILE)
        own_ref[span, :] = product(grad_pre[span, :], w_self[...], 1, 1) + grad_ext[block].T
    for copy in outs:
        copy.wait()


def layer(tile_cols, node_feats, arrived, tile_vals, w_self, w_neigh, grad_out):
    rows, width = node_feats.shape
    like = pltpu.VMEM((rows, width), jnp.bfloat16)
    return pl.pallas_call(
        layer_kernel,
        out_shape=[
            jax.ShapeDtypeStruct((rows, width), jnp.bfloat16),
            jax.ShapeDtypeStruct((2 * width, width), jnp.bfloat16),
            jax.ShapeDtypeStruct((rows, width), jnp.float32),
        ]
        + [jax.ShapeDtypeStruct((TILE, width), jnp.bfloat16)] * 4,
        in_specs=[SMEM] + [VMEM] * 9,
        out_specs=[HBM] + [VMEM] * 6,
        scratch_shapes=[
            pltpu.VMEM((rows + 4 * TILE, width), jnp.bfloat16),
            like,
            like,
            like,
            pltpu.VMEM((width, rows), jnp.bfloat16),
            pltpu.VMEM((rows // TILE + 4, width, TILE), jnp.float32),
            pltpu.SemaphoreType.DMA((rows // (2 * TILE),)),
        ],
        compiler_params=pltpu.CompilerParams(vmem_limit_bytes=16 * 1024 * 1024),
        cost_estimate=pl.CostEstimate(flops=2 << 30, bytes_accessed=5 << 20, transcendentals=1 << 18),
        name="layer",
    )(tile_cols, node_feats, *arrived, tile_vals, w_self, w_neigh, grad_out)


def collect_kernel(index, count, own, back0, back1, back2, back3, out_hbm, out, out_sem):
    rows = own.shape[0]
    pair = 2 * TILE
    returned = jnp.concatenate([back0[...], back1[...], back2[...], back3[...]], axis=0)
    listed = [jnp.broadcast_to(listed_rows(index, count, list_of(swap)), (pair, TILE)) for swap in range(4)]
    outs = []
    for low in range(0, rows, pair):
        span = pl.ds(low, pair)
        place = lax.broadcasted_iota(jnp.int32, (pair, TILE), 0) + low
        chosen = jnp.concatenate([(row == place).astype(jnp.bfloat16) for row in listed], axis=1)
        out[span, :] = (own[span, :] + product(chosen, returned)).astype(jnp.bfloat16)
        outs += started((out.at[span], out_hbm.at[span], out_sem.at[low // pair]))
    for copy in outs:
        copy.wait()


def collect(send_index, send_count, own_grad, returned):
    rows, width = own_grad.shape
    return pl.pallas_call(
        collect_kernel,
        out_shape=jax.ShapeDtypeStruct((rows, width), jnp.bfloat16),
        in_specs=[VMEM, SMEM] + [VMEM] * 5,
        out_specs=HBM,
        scratch_shapes=[
            pltpu.VMEM((rows, width), jnp.bfloat16),
            pltpu.SemaphoreType.DMA((rows // (2 * TILE),)),
        ],
        compiler_params=PARAMS,
        cost_estimate=pl.CostEstimate(flops=2 * 512 * 1024 * 256, bytes_accessed=2 << 20, transcendentals=0),
        name="collect",
    )(send_index, send_count, own_grad, *returned)


def shards(node_feats, send_index, send_count, tile_cols, tile_vals, w_self, w_neigh, grad_out):
    rows, width = node_feats.shape
    payload = payloads(send_index, send_count, node_feats)
    arrived = [swapped(payload[swap], swap) for swap in range(4)]
    node_out, parts, own_grad, *back = layer(
        tile_cols, node_feats, arrived, tile_vals, w_self, w_neigh, grad_out
    )
    row_n = lax.axis_size(ROW)
    share = exchange(parts.reshape(row_n, 2 * width // row_n, width), ROW)
    share = share.astype(jnp.float32).sum(0).astype(jnp.bfloat16)
    share = exchange(copies_for(share, "y"), "y").astype(jnp.float32).sum(0)
    share, *back = ahead((share, *back))
    returned = [swapped(back[swap], swap) for swap in range(2)]
    share = exchange(copies_for(share, "z"), "z").sum(0)
    share = (share * float(rows * lax.axis_size(DOM)) ** (-0.5)).astype(jnp.bfloat16)
    share, returned[0], returned[1], back[2], back[3] = ahead(
        (share, returned[0], returned[1], back[2], back[3])
    )
    whole = exchange(copies_for(share, ROW), ROW).reshape(2 * width, width)
    returned += [swapped(back[2], 2), swapped(back[3], 3)]
    grad_nodes = collect(send_index, send_count, own_grad, returned)
    return (
        node_out,
        grad_nodes,
        whole[:width].astype(jnp.float32),
        whole[width:].astype(jnp.float32),
    )


def solution(mesh):
    grid = Mesh(mesh.devices.reshape(4, 8, 8, 2), DOM)
    placed = (
        P(DOM, None),
        P(DOM, None, None),
        P(DOM, None),
        P(DOM, None),
        P(DOM, None, None, None),
        P(),
        P(),
        P(DOM, None),
    )
    return jax.shard_map(
        shards,
        mesh=grid,
        in_specs=placed,
        out_specs=(P(DOM, None), P(DOM, None), P(), P()),
        check_vma=False,
    )
```

```python
import jax
import jax.numpy as jnp
from jax import lax
from jax.experimental import pallas as pl
from jax.experimental.pallas import tpu as pltpu
from jax.sharding import Mesh, PartitionSpec as P

DOM = ("z", "y", "x", "core")
ROW = ("x", "core")
TILE = 128
PARAMS = pltpu.CompilerParams(vmem_limit_bytes=16 * 1024 * 1024)
VMEM = pl.BlockSpec(memory_space=pltpu.VMEM)
HBM = pl.BlockSpec(memory_space=pltpu.HBM)
SMEM = pl.BlockSpec(memory_space=pltpu.SMEM)


def product(left, right, left_dim=1, right_dim=0):
    return lax.dot_general(
        left, right, (((left_dim,), (right_dim,)), ((), ())), preferred_element_type=jnp.float32
    )


def ahead(values):
    return lax.optimization_barrier(values)


def exchange(value, axes):
    return lax.all_to_all(value, axes, 0, 0, tiled=False)


def copies_for(share, axes):
    return jnp.broadcast_to(share, (lax.axis_size(axes),) + share.shape)


def partner(device, swap):
    if swap == 0:
        return device + (1 if device % 2 else -1)
    if swap == 1:
        return device + (2 if device // 2 % 2 else -2)
    return device ^ (2 if swap == 2 else 1)


def swapped(value, swap):
    count = lax.axis_size(DOM)
    pairs = [(device, partner(device, swap)) for device in range(count)]
    return lax.ppermute(value, DOM, [pair for pair in pairs if 0 <= pair[1] < count])


def list_of(swap):
    core, odd = lax.axis_index("core"), lax.axis_index("x") % 2
    return (1 - core, 3 - odd, 2 + odd, core)[swap]


def slot_of(swap):
    core, odd = lax.axis_index("core"), lax.axis_index("x") % 2
    return (core, 2 + odd, 3 - odd, 1 - core)[swap]


def started(*pairs):
    copies = [pltpu.make_async_copy(*pair) for pair in pairs]
    for copy in copies:
        copy.start()
    return copies


def listed_rows(index_ref, count_ref, slot):
    indices = index_ref[0, pl.ds(slot, 1), :]
    lane = lax.broadcasted_iota(jnp.int32, indices.shape, 1)
    return jnp.where(lane < count_ref[0, slot], indices, -1)


def payload_kernel(index_hbm, count_hbm, feats_hbm, *refs):
    outs, (index, count, feats, picked, sems, out_sem) = refs[:4], refs[4:]
    rows = feats.shape[0]
    index_copy, count_copy, feats_copy = started(
        (index_hbm, index, sems.at[0]), (count_hbm, count, sems.at[1]), (feats_hbm, feats, sems.at[2])
    )
    index_copy.wait()
    count_copy.wait()
    place = lax.broadcasted_iota(jnp.int32, (TILE, TILE), 1)
    chosen = []
    for swap in range(4):
        column = jnp.transpose(jnp.broadcast_to(listed_rows(index, count, list_of(swap)), (TILE, TILE)))
        chosen.append(
            jnp.concatenate(
                [(column == place + block * TILE).astype(jnp.bfloat16) for block in range(rows // TILE)], axis=1
            )
        )
    feats_copy.wait()
    copies = []
    for swap in range(4):
        picked[swap] = product(chosen[swap], feats[...]).astype(jnp.bfloat16)
        copies += started((picked.at[swap], outs[swap], out_sem.at[swap]))
    for copy in copies:
        copy.wait()


def payloads(send_index, send_count, node_feats):
    shape = jax.ShapeDtypeStruct((TILE, node_feats.shape[1]), jnp.bfloat16)
    return pl.pallas_call(
        payload_kernel,
        out_shape=[shape] * 4,
        in_specs=[HBM] * 3,
        out_specs=[HBM] * 4,
        scratch_shapes=[
            pltpu.VMEM(send_index.shape, jnp.int32),
            pltpu.SMEM(send_count.shape, jnp.int32),
            pltpu.VMEM(node_feats.shape, jnp.bfloat16),
            pltpu.VMEM((4, *shape.shape), jnp.bfloat16),
            pltpu.SemaphoreType.DMA((3,)),
            pltpu.SemaphoreType.DMA((4,)),
        ],
        compiler_params=pltpu.CompilerParams(vmem_limit_bytes=58 * 1024 * 1024),
        cost_estimate=pl.CostEstimate(flops=1 << 36, bytes_accessed=1 << 20, transcendentals=0),
        name="payload",
    )(send_index, send_count, node_feats)


def layer_kernel(
    cols, feats, got0, got1, got2, got3, vals, w_self, w_neigh, grad_out,
    node_out_hbm, parts_ref, own_ref, near_ref, far_ref, pair_ref,
    ext, agg, node_out, grad_pre, grad_agg, grad_ext, out_sem,
):
    blocks, tiles = cols.shape
    rows, width = feats.shape
    pair = 2 * TILE
    ext[0:rows, :] = feats[...]
    for swap, got in enumerate((got0, got1, got2, got3)):
        ext[pl.ds(pl.multiple_of(rows + slot_of(swap) * TILE, TILE), TILE), :] = got[...]
    grad_ext[...] = jnp.zeros_like(grad_ext)
    for r in range(blocks):
        tile_row = jnp.concatenate([vals[r, t] for t in range(tiles)], axis=1)
        picked = jnp.concatenate(
            [ext[pl.ds(pl.multiple_of(cols[r, t] * TILE, TILE), TILE), :] for t in range(tiles)], axis=0
        )
        agg[r * TILE : (r + 1) * TILE, :] = product(tile_row, picked).astype(jnp.bfloat16)
    outs = []
    for low in range(0, rows, pair):
        span = pl.ds(low, pair)
        preact = product(feats[span, :], w_self[...]) + product(agg[span, :], w_neigh[...])
        sigma = 1.0 / (1.0 + jnp.exp(-preact))
        node_out[span, :] = (preact * sigma).astype(jnp.bfloat16)
        slope = sigma * (1.0 + preact * (1.0 - sigma))
        grad_pre[span, :] = (grad_out[span, :].astype(jnp.float32) * slope).astype(jnp.bfloat16)
        outs += started((node_out.at[span], node_out_hbm.at[span], out_sem.at[low // pair]))
    grad_agg[...] = product(w_neigh[...], grad_pre[...], 1, 1).astype(jnp.bfloat16)
    parts_ref[0:width, :] = product(feats[...], grad_pre[...], 0, 0).astype(jnp.bfloat16)
    parts_ref[width:, :] = product(agg[...], grad_pre[...], 0, 0).astype(jnp.bfloat16)
    for r in range(blocks):
        grad_row = grad_agg[:, r * TILE : (r + 1) * TILE]
        for t in range(tiles):
            grad_ext[cols[r, t]] += product(grad_row, vals[r, t])
    for slot in range(2):
        near_ref[slot * TILE : (slot + 1) * TILE, :] = grad_ext[blocks + slot].T.astype(jnp.bfloat16)
    far_ref[...] = grad_ext[blocks + slot_of(1)].T.astype(jnp.bfloat16)
    pair_ref[...] = grad_ext[blocks + slot_of(2)].T.astype(jnp.bfloat16)
    for block in range(blocks):
        span = pl.ds(block * TILE, TILE)
        own_ref[span, :] = product(grad_pre[span, :], w_self[...], 1, 1) + grad_ext[block].T
    for copy in outs:
        copy.wait()


def layer(tile_cols, node_feats, arrived, tile_vals, w_self, w_neigh, grad_out):
    rows, width = node_feats.shape
    like = pltpu.VMEM((rows, width), jnp.bfloat16)
    return pl.pallas_call(
        layer_kernel,
        out_shape=[
            jax.ShapeDtypeStruct((rows, width), jnp.bfloat16),
            jax.ShapeDtypeStruct((2 * width, width), jnp.bfloat16),
            jax.ShapeDtypeStruct((rows, width), jnp.float32),
        ]
        + [jax.ShapeDtypeStruct((size, width), jnp.bfloat16) for size in (2 * TILE, TILE, TILE)],
        in_specs=[SMEM] + [VMEM] * 9,
        out_specs=[HBM] + [VMEM] * 5,
        scratch_shapes=[
            pltpu.VMEM((rows + 4 * TILE, width), jnp.bfloat16),
            like,
            like,
            like,
            pltpu.VMEM((width, rows), jnp.bfloat16),
            pltpu.VMEM((rows // TILE + 4, width, TILE), jnp.float32),
            pltpu.SemaphoreType.DMA((rows // (2 * TILE),)),
        ],
        compiler_params=PARAMS,
        cost_estimate=pl.CostEstimate(flops=2 << 30, bytes_accessed=5 << 20, transcendentals=1 << 18),
        name="layer",
    )(tile_cols, node_feats, *arrived, tile_vals, w_self, w_neigh, grad_out)


def join_kernel(near_ref, far_ref, pair_ref, far_out, pair_out):
    odd = lax.axis_index("x") % 2
    for out, ref, half in ((far_out, far_ref, odd), (pair_out, pair_ref, 1 - odd)):
        out[0:TILE, :] = ref[...]
        out[TILE:, :] = near_ref[pl.ds(pl.multiple_of(half * TILE, TILE), TILE), :]


def joined(near, far, pair):
    return pl.pallas_call(
        join_kernel,
        out_shape=[jax.ShapeDtypeStruct(near.shape, near.dtype)] * 2,
        in_specs=[VMEM] * 3,
        out_specs=[VMEM] * 2,
        compiler_params=pltpu.CompilerParams(vmem_limit_bytes=4 * 1024 * 1024),
        name="join",
    )(near, far, pair)


def collect_kernel(index, count, own, near, far, pair_rows, out_hbm, out, out_sem):
    rows = own.shape[0]
    pair = 2 * TILE
    core, odd = lax.axis_index("core"), lax.axis_index("x") % 2
    passed = jnp.where(core == odd, far[TILE:, :], pair_rows[TILE:, :])
    swapped_rows = near[pl.ds(pl.multiple_of(core * TILE, TILE), TILE), :]
    returned = jnp.concatenate([passed, far[0:TILE, :], pair_rows[0:TILE, :], swapped_rows], axis=0)
    listed = [jnp.broadcast_to(listed_rows(index, count, list_of(swap)), (pair, TILE)) for swap in range(4)]
    outs = []
    for low in range(0, rows, pair):
        span = pl.ds(low, pair)
        place = lax.broadcasted_iota(jnp.int32, (pair, TILE), 0) + low
        chosen = jnp.concatenate([(row == place).astype(jnp.bfloat16) for row in listed], axis=1)
        out[span, :] = (own[span, :] + product(chosen, returned)).astype(jnp.bfloat16)
        outs += started((out.at[span], out_hbm.at[span], out_sem.at[low // pair]))
    for copy in outs:
        copy.wait()


def collect(send_index, send_count, own_grad, near, far, pair):
    rows, width = own_grad.shape
    return pl.pallas_call(
        collect_kernel,
        out_shape=jax.ShapeDtypeStruct((rows, width), jnp.bfloat16),
        in_specs=[VMEM, SMEM] + [VMEM] * 4,
        out_specs=HBM,
        scratch_shapes=[
            pltpu.VMEM((rows, width), jnp.bfloat16),
            pltpu.SemaphoreType.DMA((rows // (2 * TILE),)),
        ],
        compiler_params=PARAMS,
        cost_estimate=pl.CostEstimate(flops=2 * 512 * 1024 * 256, bytes_accessed=2 << 20, transcendentals=0),
        name="collect",
    )(send_index, send_count, own_grad, near, far, pair)


def shards(node_feats, send_index, send_count, tile_cols, tile_vals, w_self, w_neigh, grad_out):
    rows, width = node_feats.shape
    payload = payloads(send_index, send_count, node_feats)
    arrived = [swapped(payload[swap], swap) for swap in range(4)]
    node_out, parts, own_grad, near, far, pair = layer(
        tile_cols, node_feats, arrived, tile_vals, w_self, w_neigh, grad_out
    )
    row_n = lax.axis_size(ROW)
    share = exchange(parts.reshape(row_n, 2 * width // row_n, width), ROW)
    near = swapped(near, 3)
    far, pair = joined(near, far, pair)
    share, near, far, pair = ahead((share, near, far, pair))
    share = share.astype(jnp.float32).sum(0).astype(jnp.bfloat16)
    share = exchange(copies_for(share, "y"), "y").astype(jnp.float32).sum(0)
    share, far, pair = ahead((share, far, pair))
    far = swapped(far, 1)
    share = exchange(copies_for(share, "z"), "z").sum(0)
    share = (share * float(rows * lax.axis_size(DOM)) ** (-0.5)).astype(jnp.bfloat16)
    share, far, pair = ahead((share, far, pair))
    whole = exchange(copies_for(share, ROW), ROW).reshape(2 * width, width)
    pair = swapped(pair, 2)
    grad_nodes = collect(send_index, send_count, own_grad, near, far, pair)
    return (
        node_out,
        grad_nodes,
        whole[:width].astype(jnp.float32),
        whole[width:].astype(jnp.float32),
    )


def solution(mesh):
    grid = Mesh(mesh.devices.reshape(4, 8, 8, 2), DOM)
    placed = (
        P(DOM, None),
        P(DOM, None, None),
        P(DOM, None),
        P(DOM, None),
        P(DOM, None, None, None),
        P(),
        P(),
        P(DOM, None),
    )
    return jax.shard_map(
        shards,
        mesh=grid,
        in_specs=placed,
        out_specs=(P(DOM, None), P(DOM, None), P(), P()),
        check_vma=False,
    )
```

```python
import jax
import jax.numpy as jnp
from jax import lax
from jax.experimental import pallas as pl
from jax.experimental.pallas import tpu as pltpu
from jax.sharding import Mesh, PartitionSpec as P

DOM = ("z", "y", "x", "core")
ROW = ("x", "core")
TILE = 128
PARAMS = pltpu.CompilerParams(vmem_limit_bytes=16 * 1024 * 1024)
VMEM = pl.BlockSpec(memory_space=pltpu.VMEM)
HBM = pl.BlockSpec(memory_space=pltpu.HBM)
SMEM = pl.BlockSpec(memory_space=pltpu.SMEM)


def product(left, right, left_dim=1, right_dim=0):
    return lax.dot_general(
        left, right, (((left_dim,), (right_dim,)), ((), ())), preferred_element_type=jnp.float32
    )


def ahead(values):
    return lax.optimization_barrier(values)


def exchange(value, axes):
    return lax.all_to_all(value, axes, 0, 0, tiled=False)


def copies_for(share, axes):
    return jnp.broadcast_to(share, (lax.axis_size(axes),) + share.shape)


def partner(device, swap):
    if swap == 0:
        return device + (1 if device % 2 else -1)
    if swap == 1:
        return device + (2 if device // 2 % 2 else -2)
    return device ^ (2 if swap == 2 else 1)


def swapped(value, swap):
    count = lax.axis_size(DOM)
    pairs = [(device, partner(device, swap)) for device in range(count)]
    return lax.ppermute(value, DOM, [pair for pair in pairs if 0 <= pair[1] < count])


def list_of(swap):
    core, odd = lax.axis_index("core"), lax.axis_index("x") % 2
    return (1 - core, 3 - odd, 2 + odd, core)[swap]


def slot_of(swap):
    core, odd = lax.axis_index("core"), lax.axis_index("x") % 2
    return (core, 2 + odd, 3 - odd, 1 - core)[swap]


def started(*pairs):
    copies = [pltpu.make_async_copy(*pair) for pair in pairs]
    for copy in copies:
        copy.start()
    return copies


def listed_rows(index_ref, count_ref, slot):
    indices = index_ref[0, pl.ds(slot, 1), :]
    lane = lax.broadcasted_iota(jnp.int32, indices.shape, 1)
    return jnp.where(lane < count_ref[0, slot], indices, -1)


def payload_kernel(index_hbm, count_hbm, feats_hbm, *refs):
    outs, (index, count, feats, picked, sems, out_sem) = refs[:4], refs[4:]
    rows = feats.shape[0]
    index_copy, count_copy, feats_copy = started(
        (index_hbm, index, sems.at[0]), (count_hbm, count, sems.at[1]), (feats_hbm, feats, sems.at[2])
    )
    index_copy.wait()
    count_copy.wait()
    place = lax.broadcasted_iota(jnp.int32, (TILE, TILE), 1)
    chosen = []
    for swap in range(4):
        column = jnp.transpose(jnp.broadcast_to(listed_rows(index, count, list_of(swap)), (TILE, TILE)))
        chosen.append(
            jnp.concatenate(
                [(column == place + block * TILE).astype(jnp.bfloat16) for block in range(rows // TILE)], axis=1
            )
        )
    feats_copy.wait()
    copies = []
    for swap in range(4):
        picked[swap] = product(chosen[swap], feats[...]).astype(jnp.bfloat16)
        copies += started((picked.at[swap], outs[swap], out_sem.at[swap]))
    for copy in copies:
        copy.wait()


def payloads(send_index, send_count, node_feats):
    shape = jax.ShapeDtypeStruct((TILE, node_feats.shape[1]), jnp.bfloat16)
    return pl.pallas_call(
        payload_kernel,
        out_shape=[shape] * 4,
        in_specs=[HBM] * 3,
        out_specs=[HBM] * 4,
        scratch_shapes=[
            pltpu.VMEM(send_index.shape, jnp.int32),
            pltpu.SMEM(send_count.shape, jnp.int32),
            pltpu.VMEM(node_feats.shape, jnp.bfloat16),
            pltpu.VMEM((4, *shape.shape), jnp.bfloat16),
            pltpu.SemaphoreType.DMA((3,)),
            pltpu.SemaphoreType.DMA((4,)),
        ],
        compiler_params=pltpu.CompilerParams(vmem_limit_bytes=58 * 1024 * 1024),
        cost_estimate=pl.CostEstimate(flops=1 << 36, bytes_accessed=1 << 20, transcendentals=0),
        name="payload",
    )(send_index, send_count, node_feats)


def layer_kernel(
    cols, feats, got0, got1, got2, got3, vals, w_self, w_neigh, grad_out,
    node_out_hbm, parts_ref, own_ref, near_ref, far_ref, pair_ref,
    ext, agg, node_out, grad_pre, grad_agg, grad_ext, out_sem,
):
    blocks, tiles = cols.shape
    rows, width = feats.shape
    pair = 2 * TILE
    ext[0:rows, :] = feats[...]
    for swap, got in enumerate((got0, got1, got2, got3)):
        ext[pl.ds(pl.multiple_of(rows + slot_of(swap) * TILE, TILE), TILE), :] = got[...]
    grad_ext[...] = jnp.zeros_like(grad_ext)
    for r in range(blocks):
        tile_row = jnp.concatenate([vals[r, t] for t in range(tiles)], axis=1)
        picked = jnp.concatenate(
            [ext[pl.ds(pl.multiple_of(cols[r, t] * TILE, TILE), TILE), :] for t in range(tiles)], axis=0
        )
        agg[r * TILE : (r + 1) * TILE, :] = product(tile_row, picked).astype(jnp.bfloat16)
    outs = []
    for low in range(0, rows, pair):
        span = pl.ds(low, pair)
        preact = product(feats[span, :], w_self[...]) + product(agg[span, :], w_neigh[...])
        sigma = 1.0 / (1.0 + jnp.exp(-preact))
        node_out[span, :] = (preact * sigma).astype(jnp.bfloat16)
        slope = sigma * (1.0 + preact * (1.0 - sigma))
        grad_pre[span, :] = (grad_out[span, :].astype(jnp.float32) * slope).astype(jnp.bfloat16)
        outs += started((node_out.at[span], node_out_hbm.at[span], out_sem.at[low // pair]))
    grad_agg[...] = product(w_neigh[...], grad_pre[...], 1, 1).astype(jnp.bfloat16)
    parts_ref[0:width, :] = product(feats[...], grad_pre[...], 0, 0).astype(jnp.bfloat16)
    parts_ref[width:, :] = product(agg[...], grad_pre[...], 0, 0).astype(jnp.bfloat16)
    for r in range(blocks):
        grad_row = grad_agg[:, r * TILE : (r + 1) * TILE]
        for t in range(tiles):
            grad_ext[cols[r, t]] += product(grad_row, vals[r, t])
    for slot in range(2):
        near_ref[slot * TILE : (slot + 1) * TILE, :] = grad_ext[blocks + slot].T.astype(jnp.bfloat16)
    far_ref[...] = grad_ext[blocks + slot_of(1)].T.astype(jnp.bfloat16)
    pair_ref[...] = grad_ext[blocks + slot_of(2)].T.astype(jnp.bfloat16)
    for block in range(blocks):
        span = pl.ds(block * TILE, TILE)
        own_ref[span, :] = product(grad_pre[span, :], w_self[...], 1, 1) + grad_ext[block].T
    for copy in outs:
        copy.wait()


def layer(tile_cols, node_feats, arrived, tile_vals, w_self, w_neigh, grad_out):
    rows, width = node_feats.shape
    like = pltpu.VMEM((rows, width), jnp.bfloat16)
    return pl.pallas_call(
        layer_kernel,
        out_shape=[
            jax.ShapeDtypeStruct((rows, width), jnp.bfloat16),
            jax.ShapeDtypeStruct((2 * width, width), jnp.bfloat16),
            jax.ShapeDtypeStruct((rows, width), jnp.float32),
        ]
        + [jax.ShapeDtypeStruct((size, width), jnp.bfloat16) for size in (2 * TILE, TILE, TILE)],
        in_specs=[SMEM] + [VMEM] * 9,
        out_specs=[HBM] + [VMEM] * 5,
        scratch_shapes=[
            pltpu.VMEM((rows + 4 * TILE, width), jnp.bfloat16),
            like,
            like,
            like,
            pltpu.VMEM((width, rows), jnp.bfloat16),
            pltpu.VMEM((rows // TILE + 4, width, TILE), jnp.float32),
            pltpu.SemaphoreType.DMA((rows // (2 * TILE),)),
        ],
        compiler_params=PARAMS,
        cost_estimate=pl.CostEstimate(flops=2 << 30, bytes_accessed=5 << 20, transcendentals=1 << 18),
        name="layer",
    )(tile_cols, node_feats, *arrived, tile_vals, w_self, w_neigh, grad_out)


def join_kernel(near_ref, far_ref, pair_ref, far_out, pair_out):
    odd = lax.axis_index("x") % 2
    for out, ref, half in ((far_out, far_ref, odd), (pair_out, pair_ref, 1 - odd)):
        out[0:TILE, :] = ref[...]
        out[TILE:, :] = near_ref[pl.ds(pl.multiple_of(half * TILE, TILE), TILE), :]


def joined(near, far, pair):
    return pl.pallas_call(
        join_kernel,
        out_shape=[jax.ShapeDtypeStruct(near.shape, near.dtype)] * 2,
        in_specs=[VMEM] * 3,
        out_specs=[VMEM] * 2,
        compiler_params=pltpu.CompilerParams(vmem_limit_bytes=4 * 1024 * 1024),
        name="join",
    )(near, far, pair)


def collect_kernel(index, count, own, near, far, pair_rows, out_hbm, out, out_sem):
    rows = own.shape[0]
    pair = 2 * TILE
    core, odd = lax.axis_index("core"), lax.axis_index("x") % 2
    passed = jnp.where(core == odd, far[TILE:, :], pair_rows[TILE:, :])
    swapped_rows = near[pl.ds(pl.multiple_of(core * TILE, TILE), TILE), :]
    returned = jnp.concatenate([passed, far[0:TILE, :], pair_rows[0:TILE, :], swapped_rows], axis=0)
    listed = [jnp.broadcast_to(listed_rows(index, count, list_of(swap)), (pair, TILE)) for swap in range(4)]
    outs = []
    for low in range(0, rows, pair):
        span = pl.ds(low, pair)
        place = lax.broadcasted_iota(jnp.int32, (pair, TILE), 0) + low
        chosen = jnp.concatenate([(row == place).astype(jnp.bfloat16) for row in listed], axis=1)
        out[span, :] = (own[span, :] + product(chosen, returned)).astype(jnp.bfloat16)
        outs += started((out.at[span], out_hbm.at[span], out_sem.at[low // pair]))
    for copy in outs:
        copy.wait()


def collect(send_index, send_count, own_grad, near, far, pair):
    rows, width = own_grad.shape
    return pl.pallas_call(
        collect_kernel,
        out_shape=jax.ShapeDtypeStruct((rows, width), jnp.bfloat16),
        in_specs=[VMEM, SMEM] + [VMEM] * 4,
        out_specs=HBM,
        scratch_shapes=[
            pltpu.VMEM((rows, width), jnp.bfloat16),
            pltpu.SemaphoreType.DMA((rows // (2 * TILE),)),
        ],
        compiler_params=PARAMS,
        cost_estimate=pl.CostEstimate(flops=2 * 512 * 1024 * 256, bytes_accessed=2 << 20, transcendentals=0),
        name="collect",
    )(send_index, send_count, own_grad, near, far, pair)


def shards(node_feats, send_index, send_count, tile_cols, tile_vals, w_self, w_neigh, grad_out):
    rows, width = node_feats.shape
    payload = payloads(send_index, send_count, node_feats)
    arrived = [swapped(payload[swap], swap) for swap in range(4)]
    node_out, parts, own_grad, near, far, pair = layer(
        tile_cols, node_feats, arrived, tile_vals, w_self, w_neigh, grad_out
    )
    row_n = lax.axis_size(ROW)
    share = exchange(parts.reshape(row_n, 2 * width // row_n, width), ROW)
    near = swapped(near, 3)
    far, pair = joined(near, far, pair)
    share, near, far, pair = ahead((share, near, far, pair))
    share = share.astype(jnp.float32).sum(0).astype(jnp.bfloat16)
    share = exchange(copies_for(share, "y"), "y").astype(jnp.float32).sum(0)
    share, far, pair = ahead((share, far, pair))
    far, pair = swapped(far, 1), swapped(pair, 2)
    share = exchange(copies_for(share, "z"), "z").sum(0)
    share = (share * float(rows * lax.axis_size(DOM)) ** (-0.5)).astype(jnp.bfloat16)
    share, far, pair = ahead((share, far, pair))
    whole = exchange(copies_for(share, ROW), ROW).reshape(2 * width, width)
    grad_nodes = collect(send_index, send_count, own_grad, near, far, pair)
    return (
        node_out,
        grad_nodes,
        whole[:width].astype(jnp.float32),
        whole[width:].astype(jnp.float32),
    )


def solution(mesh):
    grid = Mesh(mesh.devices.reshape(4, 8, 8, 2), DOM)
    placed = (
        P(DOM, None),
        P(DOM, None, None),
        P(DOM, None),
        P(DOM, None),
        P(DOM, None, None, None),
        P(),
        P(),
        P(DOM, None),
    )
    return jax.shard_map(
        shards,
        mesh=grid,
        in_specs=placed,
        out_specs=(P(DOM, None), P(DOM, None), P(), P()),
        check_vma=False,
    )
```
